128 devices in a mesh: row: 16 (over z, x), col: 8 (over y, core).
Axes of the slice: x: 4, y: 4, z: 4, core: 2. Of those that a mesh axis runs over, the one named last changes fastest.
Arguments:
- fine_blocks: bfloat16 [64, 32, 64, 576], P('row', 'col'), may hold values from -0.25 to 0.25
- fine_columns: int32 [64, 32, 9], P('row', 'col'), may hold values from 0 to 2047, as said below
- fine_counts: int32 [64, 32], P('row', 'col'), may hold values from 1 to 9, as said below
- prolong_blocks: bfloat16 [64, 32, 64, 256], P('row', 'col'), may hold values from -1.1953125 to 1.1953125
- prolong_columns: int32 [64, 32, 4], P('row', 'col'), may hold values from 0 to 127, as said below
- prolong_counts: int32 [64, 32], P('row', 'col'), may hold values from 1 to 4, as said below
Outputs:
- galerkin: bfloat16 [16, 8, 64, 3136], P('row', 'col')
The draws below stay inside these ranges and needn't reach their ends.
Inputs may be any that keep to these rules, and one draw needn't show every extreme that they name: `fine_columns`: entry 0 of patch (x, y) is the patch itself; entries 1 to 8 are distinct directions among the eight patches at offsets of at most one along both dimensions, in an order drawn per patch, with coordinates clamped to the grid. `fine_counts`: the patch at the low corner of each 4 x 4 tile uses all 9 blocks. `prolong_columns`: entry 0 of patch (x, y) is its own aggregate (x // 4, y // 4); the other entries are distinct aggregates inside the grid at offsets of at most one from it along both dimensions. `prolong_counts`: the patch at the low corner of each 4 x 4 tile uses all 4 blocks.
All inputs are finite; a program needn't handle non-finite values.
Results may differ from the reference program's by a relative error of at most 0.0049.
Values may be sent and summed in bfloat16 or wider, within the bound.
A program may use at most 128 MiB of HBM per device.

```python
import jax
import jax.numpy as jnp
from jax import lax

B = 64
KA = 9
KP = 4
AG = 4
PX = 4
PY = 4
FX = 64
FY = 32
CXG = 16
CYG = 8


neighbour_rows = (-1, -1, -1, 0, 0, 1, 1, 1)


neighbour_cols = (-1, 0, 1, -1, 1, -1, 0, 1)


def draw_fine_columns(key, part):
    grid_rows = jnp.arange(FX, dtype=jnp.int32)[:, None, None]
    grid_cols = jnp.arange(FY, dtype=jnp.int32)[None, :, None]
    scores = jax.random.randint(key, (FX, FY, 8), 0, 1 << 20, dtype=jnp.int32) * 8 + jnp.arange(8, dtype=jnp.int32)
    order = jnp.argsort(scores, axis=-1)[..., :KA - 1]
    target_row = jnp.clip(grid_rows + jnp.take(jnp.array(neighbour_rows, jnp.int32), order), 0, FX - 1)
    target_col = jnp.clip(grid_cols + jnp.take(jnp.array(neighbour_cols, jnp.int32), order), 0, FY - 1)
    itself = grid_rows * FY + grid_cols + jnp.zeros((FX, FY, 1), jnp.int32)
    return jnp.concatenate([itself, target_row * FY + target_col], axis=-1).astype(jnp.int32)


def corner_mask():
    return (jnp.arange(FX)[:, None] % PX == 0) & (jnp.arange(FY)[None, :] % PY == 0)


def draw_fine_counts(key, part):
    first_key, second_key = jax.random.split(key)
    level = jax.random.randint(first_key, (FX // PX, FY // PY), 1, KA + 1, dtype=jnp.int32)
    lowest = jnp.repeat(jnp.repeat(level, PX, axis=0), PY, axis=1)
    counts = jax.random.randint(second_key, (FX, FY), lowest, KA + 1, dtype=jnp.int32)
    return jnp.where(corner_mask(), KA, counts).astype(jnp.int32)


def draw_prolong_columns(key, part):
    agg_row = (jnp.arange(FX, dtype=jnp.int32) // AG)[:, None, None]
    agg_col = (jnp.arange(FY, dtype=jnp.int32) // AG)[None, :, None]
    step_rows = jnp.array(neighbour_rows, jnp.int32)
    step_cols = jnp.array(neighbour_cols, jnp.int32)
    reach_row = agg_row + step_rows
    reach_col = agg_col + step_cols
    inside = (reach_row >= 0) & (reach_row < CXG) & (reach_col >= 0) & (reach_col < CYG)
    scores = jax.random.randint(key, (FX, FY, 8), 0, 1 << 20, dtype=jnp.int32) * 8 + jnp.arange(8, dtype=jnp.int32)
    scores = scores + jnp.where(inside, 0, 1 << 24)
    order = jnp.argsort(scores, axis=-1)[..., :KP - 1]
    target_row = agg_row + jnp.take(step_rows, order)
    target_col = agg_col + jnp.take(step_cols, order)
    itself = agg_row * CYG + agg_col + jnp.zeros((FX, FY, 1), jnp.int32)
    return jnp.concatenate([itself, target_row * CYG + target_col], axis=-1).astype(jnp.int32)


def draw_prolong_counts(key, part):
    counts = jax.random.randint(key, (FX, FY), 1, KP + 1, dtype=jnp.int32)
    return jnp.where(corner_mask(), KP, counts).astype(jnp.int32)


def shard_levels(key, dims, shards, smallest, top_value):
    loudness, own = 1.0, jax.random.fold_in(key, 6)
    for axis_at, blocks in shards:
        draws = jnp.exp(jax.random.uniform(jax.random.fold_in(own, axis_at), (blocks,), jnp.float32, smallest / len(shards), top_value / len(shards)))
        loudness = loudness * jnp.repeat(draws, dims[axis_at] // blocks).reshape([-1 if axis == axis_at else 1 for axis in range(len(dims))])
    return loudness


def normal_values(own_key, shape, width, reach, cuts=(), held_as=jnp.bfloat16):
    drawn = jax.random.normal(own_key, shape, jnp.float32) * width
    if len(cuts) > 0:
        drawn = shard_levels(own_key, shape, cuts, -0.22, 0.18) * drawn
    return jnp.clip(drawn, min=-reach, max=reach).astype(held_as)


def setup_inputs(seed: int = 0) -> dict:
    seeds = jax.random.split(jax.random.key(seed), 7)
    return {
        "fine_blocks": normal_values(seeds[0], (FX, FY, B, KA * B), (KA * B) ** -0.5, 0.25, ((0, 16), (1, 8))),
        "fine_columns": draw_fine_columns(jax.random.fold_in(seeds[6], 71), 0),
        "fine_counts": draw_fine_counts(jax.random.fold_in(seeds[6], 71), 0),
        "prolong_blocks": normal_values(seeds[3], (FX, FY, B, KP * B), 0.2, 1.1953125, ((0, 16), (1, 8))),
        "prolong_columns": draw_prolong_columns(jax.random.fold_in(seeds[6], 71), 0),
        "prolong_counts": draw_prolong_counts(jax.random.fold_in(seeds[6], 71), 0),
    }


def regroup(values):
    rest = values.shape[2:]
    return values.reshape((AG, CYG, AG) + rest).swapaxes(0, 1).reshape((CYG, AG * AG) + rest)


def int_starts(values):
    return tuple(jnp.asarray(value, jnp.int32) for value in values)


def reference(fine_blocks, fine_columns, fine_counts, prolong_blocks, prolong_columns, prolong_counts):
    blocks = jnp.arange(KA, dtype=jnp.int32)
    entries = jnp.arange(KP, dtype=jnp.int32)
    fine_grid = jnp.where((blocks[None, None, :] < fine_counts[:, :, None])[:, :, None, :, None],
                          fine_blocks.reshape(FX, FY, B, KA, B), jnp.zeros((), jnp.bfloat16))
    prolong = jnp.where((entries[None, None, :] < prolong_counts[:, :, None])[:, :, None, :, None],
                        prolong_blocks.reshape(FX, FY, B, KP, B), jnp.zeros((), jnp.bfloat16))
    prolong_flat = prolong.reshape(FX * FY, B, KP, B)
    codes_flat = prolong_columns.reshape(FX * FY, KP)
    window = jnp.arange(25, dtype=jnp.int32)
    nearby = jnp.arange(9, dtype=jnp.int32)
    columns_of = jnp.arange(CYG, dtype=jnp.int32)

    def one_row(partial_value, agg_row):
        first_patch = agg_row * AG
        local_a = regroup(lax.dynamic_slice_in_dim(fine_grid, first_patch, AG, 0))
        targets = regroup(lax.dynamic_slice_in_dim(fine_columns, first_patch, AG, 0))
        near_p = jnp.take(prolong_flat, targets, axis=0)
        near_codes = jnp.take(codes_flat, targets, axis=0)
        term_blocks = jnp.einsum("gnakb,gnkbqc->gnkqac", local_a.astype(jnp.float32), near_p.astype(jnp.float32),
                                 precision=lax.Precision.HIGHEST)
        window_slot = (near_codes // CYG - agg_row + 2) * 5 + near_codes % CYG - columns_of[:, None, None, None] + 2
        select = (window_slot[..., None] == window).astype(jnp.float32)
        product = jnp.einsum("gnkqj,gnkqac->gnjac", select, term_blocks,
                             precision=lax.Precision.HIGHEST).astype(jnp.bfloat16)
        own_p = regroup(lax.dynamic_slice_in_dim(prolong, first_patch, AG, 0))
        own_codes = regroup(lax.dynamic_slice_in_dim(prolong_columns, first_patch, AG, 0))
        home_slot = (own_codes // CYG - agg_row + 1) * 3 + own_codes % CYG - columns_of[:, None, None] + 1
        spread = (home_slot[..., None] == nearby).astype(jnp.float32)
        dense_p = jnp.einsum("gnpi,gnbpc->gnibc", spread, own_p.astype(jnp.float32),
                             precision=lax.Precision.HIGHEST).astype(jnp.bfloat16)
        contrib = jnp.einsum("gniba,gnjbc->giajc", dense_p.astype(jnp.float32), product.astype(jnp.float32),
                             precision=lax.Precision.HIGHEST).reshape(CYG, 3, 3, B, 5, 5, B)
        for downward in range(3):
            for sideways in range(3):
                corner_at = int_starts((agg_row + downward, sideways, 0, 2 - downward, 2 - sideways, 0))
                current = lax.dynamic_slice(partial_value, corner_at, (1, CYG, B, 5, 5, B))
                partial_value = lax.dynamic_update_slice(partial_value, current + contrib[:, downward, sideways][None], corner_at)
        return partial_value, None

    partial_value = jnp.zeros((CXG + 2, CYG + 2, B, 7, 7, B), jnp.float32)
    partial_value, unused = lax.scan(one_row, partial_value, jnp.arange(CXG, dtype=jnp.int32))
    return partial_value[1:CXG + 1, 1:CYG + 1].reshape(CXG, CYG, B, 49 * B).astype(jnp.bfloat16)
```

```python
import functools

import jax
import jax.numpy as jnp
from jax import lax
from jax.experimental import pallas as pl
from jax.experimental.pallas import tpu as pltpu
from jax.sharding import PartitionSpec as P

MESH = pl.DeviceIdType.MESH
F32 = jnp.float32
BF16 = jnp.bfloat16

B = 64
KA = 9
KP = 4
AG = 4
PATCHES = AG * AG
UNUSED = 15
PT_ROWS = KP * B + 16
ORDER = {-1: 0, 1: 1, 0: 2}
WIDE = 26 * B
FULL = 36 * B
R_ROWS = 17 * B


def dot_nn(a, b):
    return lax.dot_general(a, b, (((1,), (0,)), ((), ())), preferred_element_type=F32)


def dot_nt(a, b):
    return lax.dot_general(a, b, (((1,), (1,)), ((), ())), preferred_element_type=F32)


def term_row(down, side):
    return (ORDER[side] * 3 + ORDER[down]) * B


def home(down, side):
    return (side + 1) * 3 + down + 1


def window_row(down, side):
    return (1 + side * 5 + down) * B


def swapped(x):
    return pltpu.roll(x.astype(F32), B, 1)


def slot_parts(x_ref, lanes, width):
    codes = x_ref[KP * B : PT_ROWS, lanes].astype(F32)
    spread = [
        jnp.broadcast_to(codes[p : p + 1], (16, width)).astype(BF16) for p in range(KP)
    ]
    blocks = [x_ref[p * B : (p + 1) * B, lanes].reshape(4, 16, width) for p in range(KP)]
    return spread, blocks


def chosen(spread, blocks, slots, code):
    total = None
    for p in slots:
        part = jnp.where((spread[p] == code)[None], blocks[p], jnp.zeros_like(blocks[p]))
        total = part if total is None else total + part
    return total.reshape(B, total.shape[-1])


def dense(x_ref, lanes, width, places, zeros):
    spread, blocks = slot_parts(x_ref, lanes, width)
    for down in (-1, 0, 1):
        for side in (-1, 0, 1):
            code = home(down, side)
            slots = range(KP) if code == 4 else range(1, KP)
            value = chosen(spread, blocks, slots, jnp.array(code, BF16))
            for ref, row, at in places(down, side):
                ref[row : row + B, at] = value
    for ref, row, at in zeros:
        ref[row : row + B, at] = jnp.zeros((B, width), BF16)


def blank_rows(ref, at, downs):
    rows = [0, 16 * B] + [window_row(d, s) for s in range(3) for d in downs]
    return [(ref, row, at) for row in rows]


def kernel(
    p_hbm, a_hbm, acode_ref, pcode_ref, out_ref,
    pv, av, ptx, edge_l, edge_r, halo_t, halo_b, halo_l, halo_r,
    pass_l, pass_r, corner_l, corner_r,
    pdt, aw, q_own, q_l, q_r, r_own, r_l, r_r, c_side, c_mid,
    send_l, send_r, got_l, got_r, send_rows, e_mid, got_u, got_d,
    in_sem, send_sem, recv_sem,
):
    row, col = lax.axis_index("row"), lax.axis_index("col")
    rows, cols = lax.axis_size("row"), lax.axis_size("col")
    up = {"row": lax.rem(row + rows - 1, rows)}
    down = {"row": lax.rem(row + 1, rows)}
    left = {"col": lax.rem(col + cols - 1, cols)}
    right = {"col": lax.rem(col + 1, cols)}

    p_in = pltpu.make_async_copy(p_hbm, pv, in_sem.at[0])
    a_in = pltpu.make_async_copy(a_hbm, av, in_sem.at[1])
    p_in.start()
    a_in.start()
    barrier = pltpu.get_barrier_semaphore()
    for peer in (up, down, left, right):
        pl.semaphore_signal(barrier, inc=1, device_id=peer, device_id_type=MESH)

    def remote(number, src, dst, peer):
        return pltpu.make_async_remote_copy(
            src_ref=src,
            dst_ref=dst,
            send_sem=send_sem.at[number],
            recv_sem=recv_sem.at[number],
            device_id=peer,
            device_id_type=MESH,
        )

    eye = (
        lax.broadcasted_iota(jnp.int32, (256, 256), 0)
        == lax.broadcasted_iota(jnp.int32, (256, 256), 1)
    ).astype(F32).astype(BF16)
    p_in.wait()
    for side, edge in ((0, edge_l), (AG - 1, edge_r)):
        edge[0 : KP * B, :] = dot_nt(eye, pv[:, side].reshape(256, 256)).astype(BF16)
    edge_l[KP * B :, :] = pcode_ref[:, 1024:1280]
    edge_r[KP * B :, :] = pcode_ref[:, 1280:1536]
    for u in range(AG):
        ptx[0 : KP * B, u * 256 : (u + 1) * 256] = dot_nt(
            eye, pv[u].reshape(256, 256)
        ).astype(BF16)
    ptx[KP * B :, :] = pcode_ref[:, 0:1024]

    pl.semaphore_wait(barrier, 4)
    to_up = remote(0, ptx.at[:, 0:256], halo_b, up)
    to_down = remote(1, ptx.at[:, 768:1024], halo_t, down)
    to_left = remote(2, edge_l, halo_r, left)
    to_right = remote(3, edge_r, halo_l, right)
    for copy in (to_up, to_down, to_left, to_right):
        copy.start()

    def own_dense(u, carry):
        lanes = pl.ds(pl.multiple_of(u * 256, 256), 256)
        dense(
            ptx, lanes, 256,
            lambda d, s: [
                (pdt, term_row(d, s), lanes),
                (r_own, window_row(d + 2, s + 1), lanes),
            ],
            blank_rows(r_own, lanes, (0, 4)),
        )
        return carry

    lax.fori_loop(0, AG, own_dense, 0)

    a_in.wait()
    lane = lax.broadcasted_iota(jnp.int32, (1, 128), 1)
    tiles = ((1, 2), (3, 4), (0, 5))

    def strip(u, carry):
        for v in range(AG):
            wide = [av[u, v, :, 128 * t : 128 * (t + 1)] for t in range(4)]
            last = av[u, v, :, 512:576]
            wide.append(jnp.concatenate([last, jnp.zeros_like(last)], axis=1))
            wide = wide + [swapped(w).astype(BF16) for w in wide]
            wide = [w.reshape(4, 16, 128) for w in wide]
            codes = acode_ref[u * AG + v]
            for at, pair in enumerate(tiles):
                sides = [target - 1 - v for target in pair]
                for dr in (-1, 0, 1):
                    here = (u + dr + 1, pl.ds((1 - dr) * 256 + v * B, B), pl.ds(at * 128, 128))
                    wanted = [(dr + 1) * 3 + dc + 1 if abs(dc) <= 1 else 99 for dc in sides]
                    if wanted == [99, 99]:
                        aw[here] = jnp.zeros((B, 128), BF16)
                        continue
                    match = jnp.where(
                        codes == jnp.where(lane < B, wanted[0], wanted[1]).astype(F32), 1.0, 0.0
                    )
                    total = None
                    for t in range(10):
                        if wanted[0] == 99 and t == 4 or wanted[1] == 99 and t == 9:
                            continue
                        mask = jnp.broadcast_to(match[t : t + 1], (16, 128)).astype(BF16)
                        part = mask[None] * wide[t]
                        total = part if total is None else total + part
                    aw[here] = total.reshape(B, 128)
        return carry

    lax.fori_loop(0, AG, strip, 0)

    def row_of_targets(w):
        first, last = max(w - 1, 0), min(w + 1, AG - 1)
        got = dot_nn(
            pdt[:, first * 256 : (last + 1) * 256],
            aw[w + 1, (first - w + 1) * 256 : (last - w + 2) * 256, :],
        )
        place = w if 0 <= w < AG else (AG if w < 0 else AG + 1)
        q_own[:, place * 256 : (place + 1) * 256] = got[:, 0:256].astype(BF16)
        return got[:, 256:384]

    half = lane < B
    for at, (w0, w1) in enumerate(((0, 1), (2, 3), (-1, 4))):
        x, y = row_of_targets(w0), row_of_targets(w1)
        lanes = slice(at * 128, (at + 1) * 128)
        q_l[:, lanes] = jnp.where(half, x, pltpu.roll(y, B, 1)).astype(BF16)
        q_r[:, lanes] = jnp.where(half, pltpu.roll(x, B, 1), y).astype(BF16)

    c_side[:, 0:256] = jnp.zeros((384, 256), F32)
    c_side[:, 1280:WIDE] = jnp.zeros((384, WIDE - 1280), F32)
    c_mid[:, 0:384] = jnp.zeros((192, 384), F32)
    c_mid[:, 1408:WIDE] = jnp.zeros((192, WIDE - 1408), F32)
    c_side[:, 256:1280] = dot_nt(q_own[0:384, 0:1024], r_own[0:1024, 0:1024])
    c_mid[:, 384:1408] = dot_nt(q_own[384:576, 0:1024], r_own[64:1088, 0:1024])

    to_down.wait_recv()
    to_up.wait_recv()
    for rows_16 in range(PT_ROWS // 16):
        at = slice(rows_16 * 16, (rows_16 + 1) * 16)
        pass_l[at, :] = jnp.where(
            half, halo_t[at, 0:128].astype(F32), swapped(halo_b[at, 0:128])
        ).astype(BF16)
        pass_r[at, :] = jnp.where(
            half, swapped(halo_t[at, 128:256]), halo_b[at, 128:256].astype(F32)
        ).astype(BF16)
    corner_to_left = remote(4, pass_l, corner_r, left)
    corner_to_right = remote(5, pass_r, corner_l, right)
    corner_to_left.start()
    corner_to_right.start()

    for halo, shift, blanks, first in ((halo_t, 1, (3, 4), 1024), (halo_b, 3, (0, 1), 1280)):
        at = slice(first, first + 256)
        dense(
            halo, slice(0, 256), 256,
            lambda d, s: [(r_own, window_row(d + shift, s + 1), at)],
            blank_rows(r_own, at, blanks),
        )
    to_left.wait_recv()
    to_right.wait_recv()
    for halo, ref in ((halo_l, r_l), (halo_r, r_r)):
        at = slice(0, 256)
        dense(
            halo, at, 256,
            lambda d, s: [(ref, window_row(d + 2, s + 1), at)],
            blank_rows(ref, at, (0, 4)),
        )
    c_side[:, 256:1280] += dot_nt(q_own[0:384, 1024:1536], r_own[0:1024, 1024:1536])

    corner_to_left.wait_recv()
    corner_to_right.wait_recv()
    for corner, ref in ((corner_l, r_l), (corner_r, r_r)):
        spread, blocks = slot_parts(corner, slice(0, 128), 128)
        for side in (-1, 0, 1):
            for j in range(5):
                above, below = j - 1, j - 3
                codes = [home(d, side) if abs(d) <= 1 else 99 for d in (above, below)]
                code = jnp.where(half, codes[0], codes[1]).astype(F32).astype(BF16)
                row_at = window_row(j, side + 1)
                ref[row_at : row_at + B, 256:384] = chosen(spread, blocks, range(KP), code)
        for row_at in (0, 16 * B):
            ref[row_at : row_at + B, 256:384] = jnp.zeros((B, 128), BF16)
    c_side[:, 0:1024] += dot_nt(q_l[0:384, :], r_l[64:1088, :])
    c_side[:, 640:WIDE] += dot_nt(q_r[0:384, :], r_r[64:1088, :])

    send_l[...] = c_side[0:192, :].astype(BF16)
    send_r[...] = c_side[192:384, :].astype(BF16)
    side_copies = []
    for number, at in ((6, slice(0, 128)), (8, slice(128, 192))):
        to_l = remote(number, send_l.at[at], got_r.at[at], left)
        to_r = remote(number + 1, send_r.at[at], got_l.at[at], right)
        to_l.start()
        to_r.start()
        side_copies.append((to_l, to_r))

    c_mid[:, 384:1408] += dot_nt(q_own[384:576, 1024:1536], r_own[64:1088, 1024:1536])
    c_mid[:, 0:1024] += dot_nt(q_l[384:576, :], r_l[0:1024, :])
    c_mid[:, 640:WIDE] += dot_nt(q_r[384:576, :], r_r[0:1024, :])

    def folded(at, lo, hi):
        total = None
        for ref, first in ((got_l, 0), (c_mid, 256), (got_r, 640)):
            if first <= lo and hi <= first + WIDE:
                part = ref[at, lo - first : hi - first].astype(F32)
                total = part if total is None else total + part
        return total

    spans = ((0, 256), (256, 640), (640, 1664), (1664, 1920), (1920, FULL))
    for copy in side_copies[0]:
        copy.wait_recv()
    for lo, hi in spans:
        send_rows[:, lo:hi] = folded(slice(0, 128), lo, hi).astype(BF16)
    to_u = remote(10, send_rows.at[0:64], got_d, up)
    to_d = remote(11, send_rows.at[64:128], got_u, down)
    to_u.start()
    to_d.start()
    for copy in side_copies[1]:
        copy.wait_recv()
    for lo, hi in spans:
        e_mid[:, lo:hi] = folded(slice(128, 192), lo, hi)
    to_u.wait_recv()
    to_d.wait_recv()

    for s in range(7):
        for t in range(7):
            total = None
            for ref, j in ((got_u, s), (e_mid, s - 1), (got_d, s - 2)):
                if 0 <= j < 5:
                    at = (t * 5 + j) * B
                    part = ref[:, at : at + B].astype(F32)
                    total = part if total is None else total + part
            at = (s * 7 + t) * B
            out_ref[0, 0, :, at : at + B] = total.astype(BF16)

    sent = [to_up, to_down, to_left, to_right, corner_to_left, corner_to_right, to_u, to_d]
    for copy in sent + [copy for pair in side_copies for copy in pair]:
        copy.wait_send()


def slot_codes(fine_columns, fine_counts, prolong_columns, prolong_counts):
    row, col = lax.axis_index("row"), lax.axis_index("col")
    fine_cols = AG * lax.axis_size("col")
    coarse_cols = lax.axis_size("col")
    steps = jnp.arange(AG, dtype=jnp.int32)
    patch_row = (row * AG + steps)[:, None, None]
    patch_col = (col * AG + steps)[None, :, None]
    toward = (fine_columns // fine_cols - patch_row + 1) * 3 + fine_columns % fine_cols - patch_col + 1
    used = jnp.arange(KA, dtype=jnp.int32) < fine_counts[:, :, None]
    toward = jnp.where(used, toward, UNUSED).astype(F32).reshape(PATCHES, KA)
    toward = jnp.pad(toward, ((0, 0), (0, 1)), constant_values=UNUSED).reshape(PATCHES, 5, 2)
    both = jnp.concatenate([toward, toward[:, :, ::-1]], axis=1)
    acode = jnp.broadcast_to(both[..., None], (PATCHES, 10, 2, B)).reshape(PATCHES, 10, 2 * B)

    home_slot = (prolong_columns % coarse_cols - col + 1) * 3 + prolong_columns // coarse_cols - row + 1
    used = jnp.arange(KP, dtype=jnp.int32) < prolong_counts[:, :, None]
    home_slot = jnp.where(used, home_slot, UNUSED).astype(BF16).transpose(2, 0, 1)
    order = [home_slot.reshape(KP, PATCHES), home_slot[:, :, 0], home_slot[:, :, AG - 1]]
    order = jnp.pad(jnp.concatenate(order, axis=1), ((0, 16 - KP), (0, 0)))
    pcode = jnp.broadcast_to(order[:, :, None], (16, 24, B)).reshape(16, 24 * B)
    return acode, pcode


def per_device(
    fine_blocks, fine_columns, fine_counts, prolong_blocks, prolong_columns, prolong_counts
):
    acode, pcode = slot_codes(fine_columns, fine_counts, prolong_columns, prolong_counts)
    vmem = pl.BlockSpec(memory_space=pltpu.VMEM)
    hbm = pl.BlockSpec(memory_space=pl.ANY)
    return pl.pallas_call(
        kernel,
        out_shape=jax.ShapeDtypeStruct((1, 1, B, 49 * B), BF16),
        in_specs=[hbm, hbm, vmem, vmem],
        out_specs=vmem,
        scratch_shapes=[
            pltpu.VMEM((AG, AG, B, KP * B), BF16),
            pltpu.VMEM((AG, AG, B, KA * B), BF16),
            pltpu.VMEM((PT_ROWS, 1024), BF16),
            pltpu.VMEM((PT_ROWS, 256), BF16),
            pltpu.VMEM((PT_ROWS, 256), BF16),
            pltpu.VMEM((PT_ROWS, 256), BF16),
            pltpu.VMEM((PT_ROWS, 256), BF16),
            pltpu.VMEM((PT_ROWS, 256), BF16),
            pltpu.VMEM((PT_ROWS, 256), BF16),
            pltpu.VMEM((PT_ROWS, 128), BF16),
            pltpu.VMEM((PT_ROWS, 128), BF16),
            pltpu.VMEM((PT_ROWS, 128), BF16),
            pltpu.VMEM((PT_ROWS, 128), BF16),
            pltpu.VMEM((9 * B, 1024), BF16),
            pltpu.VMEM((6, 768, 384), BF16),
            pltpu.VMEM((9 * B, 1536), BF16),
            pltpu.VMEM((9 * B, 384), BF16),
            pltpu.VMEM((9 * B, 384), BF16),
            pltpu.VMEM((R_ROWS, 1536), BF16),
            pltpu.VMEM((R_ROWS, 384), BF16),
            pltpu.VMEM((R_ROWS, 384), BF16),
            pltpu.VMEM((6 * B, WIDE), F32),
            pltpu.VMEM((3 * B, WIDE), F32),
            pltpu.VMEM((3 * B, WIDE), BF16),
            pltpu.VMEM((3 * B, WIDE), BF16),
            pltpu.VMEM((3 * B, WIDE), BF16),
            pltpu.VMEM((3 * B, WIDE), BF16),
            pltpu.VMEM((2 * B, FULL), BF16),
            pltpu.VMEM((B, FULL), F32),
            pltpu.VMEM((B, FULL), BF16),
            pltpu.VMEM((B, FULL), BF16),
            pltpu.SemaphoreType.DMA((2,)),
            pltpu.SemaphoreType.DMA((12,)),
            pltpu.SemaphoreType.DMA((12,)),
        ],
        compiler_params=pltpu.CompilerParams(
            collective_id=0, has_side_effects=True, vmem_limit_bytes=48 * 2**20
        ),
    )(prolong_blocks, fine_blocks, acode, pcode)


def solution(mesh):
    in_specs = (
        P("row", "col", None, None),
        P("row", "col", None),
        P("row", "col"),
        P("row", "col", None, None),
        P("row", "col", None),
        P("row", "col"),
    )
    return jax.shard_map(
        per_device,
        mesh=mesh,
        in_specs=in_specs,
        out_specs=P("row", "col", None, None),
        check_vma=False,
    )
```

```python
import functools

import jax
import jax.numpy as jnp
from jax import lax
from jax.experimental import pallas as pl
from jax.experimental.pallas import tpu as pltpu
from jax.sharding import PartitionSpec as P

MESH = pl.DeviceIdType.MESH
F32 = jnp.float32
BF16 = jnp.bfloat16

B = 64
KA = 9
KP = 4
AG = 4
UNUSED = 15
PT_ROWS = KP * B + 16
ORDER = {-1: 0, 1: 1, 0: 2}
WIDE = 26 * B
FULL = 36 * B
R_ROWS = 17 * B


def dot_nn(a, b):
    return lax.dot_general(a, b, (((1,), (0,)), ((), ())), preferred_element_type=F32)


def dot_nt(a, b):
    return lax.dot_general(a, b, (((1,), (1,)), ((), ())), preferred_element_type=F32)


def term_row(down, side):
    return (ORDER[side] * 3 + ORDER[down]) * B


def home(down, side):
    return (side + 1) * 3 + down + 1


def window_row(down, side):
    return (1 + side * 5 + down) * B


def swapped(x):
    return pltpu.roll(x.astype(F32), B, 1)


def slot_parts(x_ref, lanes, width):
    codes = x_ref[KP * B : PT_ROWS, lanes].astype(F32)
    spread = [
        jnp.broadcast_to(codes[p : p + 1], (16, width)).astype(BF16) for p in range(KP)
    ]
    blocks = [x_ref[p * B : (p + 1) * B, lanes].reshape(4, 16, width) for p in range(KP)]
    return spread, blocks


def chosen(spread, blocks, slots, code):
    total = None
    for p in slots:
        part = jnp.where((spread[p] == code)[None], blocks[p], jnp.zeros_like(blocks[p]))
        total = part if total is None else total + part
    return total.reshape(B, total.shape[-1])


def dense(x_ref, lanes, width, places, zeros):
    spread, blocks = slot_parts(x_ref, lanes, width)
    for down in (-1, 0, 1):
        for side in (-1, 0, 1):
            code = home(down, side)
            slots = range(KP) if code == 4 else range(1, KP)
            value = chosen(spread, blocks, slots, jnp.array(code, BF16))
            for ref, row, at in places(down, side):
                ref[row : row + B, at] = value
    for ref, row, at in zeros:
        ref[row : row + B, at] = jnp.zeros((B, width), BF16)


def blank_rows(ref, at, downs):
    rows = [0, 16 * B] + [window_row(d, s) for s in range(3) for d in downs]
    return [(ref, row, at) for row in rows]


def kernel(
    p_hbm, a_hbm, fine_columns, fine_counts, prolong_columns, prolong_counts, out_ref,
    pv, av, ptx, edge_l, edge_r, halo_t, halo_b, halo_l, halo_r,
    pass_l, pass_r, corner_l, corner_r,
    pdt, aw, q_own, q_l, q_r, r_own, r_l, r_r, c_side, c_mid,
    send_l, send_r, got_l, got_r, send_rows, e_mid, got_u, got_d,
    in_sem, send_sem, recv_sem,
):
    row, col = lax.axis_index("row"), lax.axis_index("col")
    rows, cols = lax.axis_size("row"), lax.axis_size("col")
    fine_cols = AG * cols
    up = {"row": lax.rem(row + rows - 1, rows)}
    down = {"row": lax.rem(row + 1, rows)}
    left = {"col": lax.rem(col + cols - 1, cols)}
    right = {"col": lax.rem(col + 1, cols)}

    p_in = pltpu.make_async_copy(p_hbm, pv, in_sem.at[0])
    a_in = pltpu.make_async_copy(a_hbm, av, in_sem.at[1])
    p_in.start()
    a_in.start()
    barrier = pltpu.get_barrier_semaphore()
    for peer in (up, down, left, right):
        pl.semaphore_signal(barrier, inc=1, device_id=peer, device_id_type=MESH)

    def remote(number, src, dst, peer):
        return pltpu.make_async_remote_copy(
            src_ref=src,
            dst_ref=dst,
            send_sem=send_sem.at[number],
            recv_sem=recv_sem.at[number],
            device_id=peer,
            device_id_type=MESH,
        )

    eye = (
        lax.broadcasted_iota(jnp.int32, (256, 256), 0)
        == lax.broadcasted_iota(jnp.int32, (256, 256), 1)
    ).astype(F32).astype(BF16)
    lane = lax.broadcasted_iota(jnp.int32, (1, 128), 1)
    line = lax.broadcasted_iota(jnp.int32, (16, 128), 0)
    half = lane < B

    def home_code(u, v, p):
        number = prolong_columns[u, v, p]
        code = (lax.bitwise_and(number, cols - 1) - col + 1) * 3 - row + 1
        code += lax.shift_right_logical(number, cols.bit_length() - 1)
        return jnp.where(p < prolong_counts[u, v], code, UNUSED)

    codes = {(u, v): [home_code(u, v, p) for p in range(KP)] for u in range(AG) for v in range(AG)}

    def code_tile(ref, at, first, second):
        tile = jnp.zeros((16, 128), jnp.int32)
        for p in range(KP):
            tile = jnp.where(line == p, jnp.where(half, codes[first][p], codes[second][p]), tile)
        ref[KP * B :, at * 128 : (at + 1) * 128] = tile.astype(F32).astype(BF16)

    for u in range(AG):
        code_tile(ptx, 2 * u, (u, 0), (u, 1))
        code_tile(ptx, 2 * u + 1, (u, 2), (u, 3))
    for side, edge in ((0, edge_l), (AG - 1, edge_r)):
        code_tile(edge, 0, (0, side), (1, side))
        code_tile(edge, 1, (2, side), (3, side))
    p_in.wait()
    for side, edge in ((0, edge_l), (AG - 1, edge_r)):
        edge[0 : KP * B, :] = dot_nt(eye, pv[:, side].reshape(256, 256)).astype(BF16)
    for u in range(AG):
        ptx[0 : KP * B, u * 256 : (u + 1) * 256] = dot_nt(
            eye, pv[u].reshape(256, 256)
        ).astype(BF16)

    pl.semaphore_wait(barrier, 4)
    to_up = remote(0, ptx.at[:, 0:256], halo_b, up)
    to_down = remote(1, ptx.at[:, 768:1024], halo_t, down)
    to_left = remote(2, edge_l, halo_r, left)
    to_right = remote(3, edge_r, halo_l, right)
    for copy in (to_up, to_down, to_left, to_right):
        copy.start()

    def own_dense(u, carry):
        lanes = pl.ds(pl.multiple_of(u * 256, 256), 256)
        dense(
            ptx, lanes, 256,
            lambda d, s: [
                (pdt, term_row(d, s), lanes),
                (r_own, window_row(d + 2, s + 1), lanes),
            ],
            blank_rows(r_own, lanes, (0, 4)),
        )
        return carry

    lax.fori_loop(0, AG, own_dense, 0)

    a_in.wait()
    tiles = ((1, 2), (3, 4), (0, 5))

    def toward_code(u, v, k):
        number = fine_columns[u, v, k]
        code = (lax.shift_right_logical(number, fine_cols.bit_length() - 1) - row * AG - u) * 3
        code += lax.bitwise_and(number, fine_cols - 1) - col * AG - v + 4
        return jnp.where(k < fine_counts[u, v], code, UNUSED)

    def strip(u, carry):
        for v in range(AG):
            wide = [av[u, v, :, 128 * t : 128 * (t + 1)] for t in range(4)]
            last = av[u, v, :, 512:576]
            wide.append(jnp.concatenate([last, jnp.zeros_like(last)], axis=1))
            wide = wide + [swapped(w).astype(BF16) for w in wide]
            wide = [w.reshape(4, 16, 128) for w in wide]
            codes = jnp.full((16, 128), UNUSED, jnp.int32)
            toward = [toward_code(u, v, k) for k in range(KA)] + [UNUSED]
            for t in range(5):
                one, two = toward[2 * t], toward[2 * t + 1]
                codes = jnp.where(line == t, jnp.where(half, one, two), codes)
                codes = jnp.where(line == t + 5, jnp.where(half, two, one), codes)
            for at, pair in enumerate(tiles):
                sides = [target - 1 - v for target in pair]
                for dr in (-1, 0, 1):
                    here = (u + dr + 1, pl.ds((1 - dr) * 256 + v * B, B), pl.ds(at * 128, 128))
                    wanted = [(dr + 1) * 3 + dc + 1 if abs(dc) <= 1 else 99 for dc in sides]
                    if wanted == [99, 99]:
                        aw[here] = jnp.zeros((B, 128), BF16)
                        continue
                    match = jnp.where(
                        codes == jnp.where(half, wanted[0], wanted[1]), 1.0, 0.0
                    )
                    total = None
                    for t in range(10):
                        if wanted[0] == 99 and t == 4 or wanted[1] == 99 and t == 9:
                            continue
                        mask = jnp.broadcast_to(match[t : t + 1], (16, 128)).astype(BF16)
                        part = mask[None] * wide[t]
                        total = part if total is None else total + part
                    aw[here] = total.reshape(B, 128)
        return carry

    lax.fori_loop(0, AG, strip, 0)

    def row_of_targets(w):
        first, last = max(w - 1, 0), min(w + 1, AG - 1)
        got = dot_nn(
            pdt[:, first * 256 : (last + 1) * 256],
            aw[w + 1, (first - w + 1) * 256 : (last - w + 2) * 256, :],
        )
        place = w if 0 <= w < AG else (AG if w < 0 else AG + 1)
        q_own[:, place * 256 : (place + 1) * 256] = got[:, 0:256].astype(BF16)
        return got[:, 256:384]

    for at, (w0, w1) in enumerate(((0, 1), (2, 3), (-1, 4))):
        x, y = row_of_targets(w0), row_of_targets(w1)
        lanes = slice(at * 128, (at + 1) * 128)
        q_l[:, lanes] = jnp.where(half, x, pltpu.roll(y, B, 1)).astype(BF16)
        q_r[:, lanes] = jnp.where(half, pltpu.roll(x, B, 1), y).astype(BF16)

    c_side[:, 0:256] = jnp.zeros((384, 256), F32)
    c_side[:, 1280:WIDE] = jnp.zeros((384, WIDE - 1280), F32)
    c_mid[:, 0:384] = jnp.zeros((192, 384), F32)
    c_mid[:, 1408:WIDE] = jnp.zeros((192, WIDE - 1408), F32)
    c_side[:, 256:1280] = dot_nt(q_own[0:384, 0:1024], r_own[0:1024, 0:1024])
    c_mid[:, 384:1408] = dot_nt(q_own[384:576, 0:1024], r_own[64:1088, 0:1024])

    to_down.wait_recv()
    to_up.wait_recv()
    for rows_16 in range(PT_ROWS // 16):
        at = slice(rows_16 * 16, (rows_16 + 1) * 16)
        pass_l[at, :] = jnp.where(
            half, halo_t[at, 0:128].astype(F32), swapped(halo_b[at, 0:128])
        ).astype(BF16)
        pass_r[at, :] = jnp.where(
            half, swapped(halo_t[at, 128:256]), halo_b[at, 128:256].astype(F32)
        ).astype(BF16)
    corner_to_left = remote(4, pass_l, corner_r, left)
    corner_to_right = remote(5, pass_r, corner_l, right)
    corner_to_left.start()
    corner_to_right.start()

    for halo, shift, blanks, first in ((halo_t, 1, (3, 4), 1024), (halo_b, 3, (0, 1), 1280)):
        at = slice(first, first + 256)
        dense(
            halo, slice(0, 256), 256,
            lambda d, s: [(r_own, window_row(d + shift, s + 1), at)],
            blank_rows(r_own, at, blanks),
        )
    to_left.wait_recv()
    to_right.wait_recv()
    for halo, ref in ((halo_l, r_l), (halo_r, r_r)):
        at = slice(0, 256)
        dense(
            halo, at, 256,
            lambda d, s: [(ref, window_row(d + 2, s + 1), at)],
            blank_rows(ref, at, (0, 4)),
        )
    c_side[:, 256:1280] += dot_nt(q_own[0:384, 1024:1536], r_own[0:1024, 1024:1536])

    corner_to_left.wait_recv()
    corner_to_right.wait_recv()
    for corner, ref in ((corner_l, r_l), (corner_r, r_r)):
        spread, blocks = slot_parts(corner, slice(0, 128), 128)
        for side in (-1, 0, 1):
            for j in range(5):
                above, below = j - 1, j - 3
                codes = [home(d, side) if abs(d) <= 1 else 99 for d in (above, below)]
                code = jnp.where(half, codes[0], codes[1]).astype(F32).astype(BF16)
                row_at = window_row(j, side + 1)
                ref[row_at : row_at + B, 256:384] = chosen(spread, blocks, range(KP), code)
        for row_at in (0, 16 * B):
            ref[row_at : row_at + B, 256:384] = jnp.zeros((B, 128), BF16)
    c_side[:, 0:1024] += dot_nt(q_l[0:384, :], r_l[64:1088, :])
    c_side[:, 640:WIDE] += dot_nt(q_r[0:384, :], r_r[64:1088, :])

    send_l[...] = c_side[0:192, :].astype(BF16)
    send_r[...] = c_side[192:384, :].astype(BF16)
    side_copies = []
    for number, at in ((6, slice(0, 128)), (8, slice(128, 192))):
        to_l = remote(number, send_l.at[at], got_r.at[at], left)
        to_r = remote(number + 1, send_r.at[at], got_l.at[at], right)
        to_l.start()
        to_r.start()
        side_copies.append((to_l, to_r))

    c_mid[:, 384:1408] += dot_nt(q_own[384:576, 1024:1536], r_own[64:1088, 1024:1536])
    c_mid[:, 0:1024] += dot_nt(q_l[384:576, :], r_l[0:1024, :])
    c_mid[:, 640:WIDE] += dot_nt(q_r[384:576, :], r_r[0:1024, :])

    def folded(at, lo, hi):
        total = None
        for ref, first in ((got_l, 0), (c_mid, 256), (got_r, 640)):
            if first <= lo and hi <= first + WIDE:
                part = ref[at, lo - first : hi - first].astype(F32)
                total = part if total is None else total + part
        return total

    spans = ((0, 256), (256, 640), (640, 1664), (1664, 1920), (1920, FULL))
    for copy in side_copies[0]:
        copy.wait_recv()
    for lo, hi in spans:
        send_rows[:, lo:hi] = folded(slice(0, 128), lo, hi).astype(BF16)
    to_u = remote(10, send_rows.at[0:64], got_d, up)
    to_d = remote(11, send_rows.at[64:128], got_u, down)
    to_u.start()
    to_d.start()
    for copy in side_copies[1]:
        copy.wait_recv()
    for lo, hi in spans:
        e_mid[:, lo:hi] = folded(slice(128, 192), lo, hi)
    to_u.wait_recv()
    to_d.wait_recv()

    for s in range(7):
        for t in range(7):
            total = None
            for ref, j in ((got_u, s), (e_mid, s - 1), (got_d, s - 2)):
                if 0 <= j < 5:
                    at = (t * 5 + j) * B
                    part = ref[:, at : at + B].astype(F32)
                    total = part if total is None else total + part
            at = (s * 7 + t) * B
            out_ref[0, 0, :, at : at + B] = total.astype(BF16)

    sent = [to_up, to_down, to_left, to_right, corner_to_left, corner_to_right, to_u, to_d]
    for copy in sent + [copy for pair in side_copies for copy in pair]:
        copy.wait_send()


def per_device(
    fine_blocks, fine_columns, fine_counts, prolong_blocks, prolong_columns, prolong_counts
):
    vmem = pl.BlockSpec(memory_space=pltpu.VMEM)
    smem = pl.BlockSpec(memory_space=pltpu.SMEM)
    hbm = pl.BlockSpec(memory_space=pl.ANY)
    return pl.pallas_call(
        kernel,
        out_shape=jax.ShapeDtypeStruct((1, 1, B, 49 * B), BF16),
        in_specs=[hbm, hbm, smem, smem, smem, smem],
        out_specs=vmem,
        scratch_shapes=[
            pltpu.VMEM((AG, AG, B, KP * B), BF16),
            pltpu.VMEM((AG, AG, B, KA * B), BF16),
            pltpu.VMEM((PT_ROWS, 1024), BF16),
            pltpu.VMEM((PT_ROWS, 256), BF16),
            pltpu.VMEM((PT_ROWS, 256), BF16),
            pltpu.VMEM((PT_ROWS, 256), BF16),
            pltpu.VMEM((PT_ROWS, 256), BF16),
            pltpu.VMEM((PT_ROWS, 256), BF16),
            pltpu.VMEM((PT_ROWS, 256), BF16),
            pltpu.VMEM((PT_ROWS, 128), BF16),
            pltpu.VMEM((PT_ROWS, 128), BF16),
            pltpu.VMEM((PT_ROWS, 128), BF16),
            pltpu.VMEM((PT_ROWS, 128), BF16),
            pltpu.VMEM((9 * B, 1024), BF16),
            pltpu.VMEM((6, 768, 384), BF16),
            pltpu.VMEM((9 * B, 1536), BF16),
            pltpu.VMEM((9 * B, 384), BF16),
            pltpu.VMEM((9 * B, 384), BF16),
            pltpu.VMEM((R_ROWS, 1536), BF16),
            pltpu.VMEM((R_ROWS, 384), BF16),
            pltpu.VMEM((R_ROWS, 384), BF16),
            pltpu.VMEM((6 * B, WIDE), F32),
            pltpu.VMEM((3 * B, WIDE), F32),
            pltpu.VMEM((3 * B, WIDE), BF16),
            pltpu.VMEM((3 * B, WIDE), BF16),
            pltpu.VMEM((3 * B, WIDE), BF16),
            pltpu.VMEM((3 * B, WIDE), BF16),
            pltpu.VMEM((2 * B, FULL), BF16),
            pltpu.VMEM((B, FULL), F32),
            pltpu.VMEM((B, FULL), BF16),
            pltpu.VMEM((B, FULL), BF16),
            pltpu.SemaphoreType.DMA((2,)),
            pltpu.SemaphoreType.DMA((12,)),
            pltpu.SemaphoreType.DMA((12,)),
        ],
        compiler_params=pltpu.CompilerParams(
            collective_id=0, has_side_effects=True, vmem_limit_bytes=60 * 2**20
        ),
    )(
        prolong_blocks, fine_blocks,
        fine_columns, fine_counts, prolong_columns, prolong_counts,
    )


def solution(mesh):
    in_specs = (
        P("row", "col", None, None),
        P("row", "col", None),
        P("row", "col"),
        P("row", "col", None, None),
        P("row", "col", None),
        P("row", "col"),
    )
    return jax.shard_map(
        per_device,
        mesh=mesh,
        in_specs=in_specs,
        out_specs=P("row", "col", None, None),
        check_vma=False,
    )
```

```python
import functools

import jax
import jax.numpy as jnp
from jax import lax
from jax.experimental import pallas as pl
from jax.experimental.pallas import tpu as pltpu
from jax.sharding import PartitionSpec as P

MESH = pl.DeviceIdType.MESH
F32 = jnp.float32
BF16 = jnp.bfloat16

B = 64
KA = 9
KP = 4
AG = 4
UNUSED = 15
PT_ROWS = KP * B + 16
ORDER = {-1: 0, 1: 1, 0: 2}
WIDE = 26 * B
FULL = 36 * B
R_ROWS = 17 * B


def dot_nn(a, b):
    return lax.dot_general(a, b, (((1,), (0,)), ((), ())), preferred_element_type=F32)


def dot_nt(a, b):
    return lax.dot_general(a, b, (((1,), (1,)), ((), ())), preferred_element_type=F32)


def term_row(down, side):
    return (ORDER[side] * 3 + ORDER[down]) * B


def home(down, side):
    return (side + 1) * 3 + down + 1


def window_row(down, side):
    return (1 + side * 5 + down) * B


def swapped(x):
    return pltpu.roll(x.astype(F32), B, 1)


def slot_parts(x_ref, lanes, width):
    codes = x_ref[KP * B : PT_ROWS, lanes].astype(F32)
    spread = [
        jnp.broadcast_to(codes[p : p + 1], (16, width)).astype(BF16) for p in range(KP)
    ]
    blocks = [x_ref[p * B : (p + 1) * B, lanes].reshape(4, 16, width) for p in range(KP)]
    return spread, blocks


def chosen(spread, blocks, slots, code):
    total = None
    for p in slots:
        part = jnp.where((spread[p] == code)[None], blocks[p], jnp.zeros_like(blocks[p]))
        total = part if total is None else total + part
    return total.reshape(B, total.shape[-1])


def dense(x_ref, lanes, width, places, zeros):
    spread, blocks = slot_parts(x_ref, lanes, width)
    for down in (-1, 0, 1):
        for side in (-1, 0, 1):
            code = home(down, side)
            slots = range(KP) if code == 4 else range(1, KP)
            value = chosen(spread, blocks, slots, jnp.array(code, BF16))
            for ref, row, at in places(down, side):
                ref[row : row + B, at] = value
    for ref, row, at in zeros:
        ref[row : row + B, at] = jnp.zeros((B, width), BF16)


def blank_rows(ref, at, downs):
    rows = [0, 16 * B] + [window_row(d, s) for s in range(3) for d in downs]
    return [(ref, row, at) for row in rows]


def kernel(
    p_hbm, a_hbm, fine_columns_hbm, fine_counts_hbm, prolong_columns_hbm, prolong_counts_hbm, out_ref,
    fine_columns, fine_counts, prolong_columns, prolong_counts,
    pv, av, ptx, edge_l, edge_r, halo_t, halo_b, halo_l, halo_r,
    pass_l, pass_r, corner_l, corner_r,
    pdt, aw, q_own, q_l, q_r, r_own, r_l, r_r, c_side, c_mid,
    send_l, send_r, got_l, got_r, send_rows, e_mid, got_u, got_d,
    in_sem, send_sem, recv_sem,
):
    row, col = lax.axis_index("row"), lax.axis_index("col")
    rows, cols = lax.axis_size("row"), lax.axis_size("col")
    fine_cols = AG * cols
    has_up, has_down, has_left, has_right = row > 0, row < rows - 1, col > 0, col < cols - 1
    up = ({"row": jnp.maximum(row - 1, 0)}, has_up, has_down)
    down = ({"row": jnp.minimum(row + 1, rows - 1)}, has_down, has_up)
    left = ({"col": jnp.maximum(col - 1, 0)}, has_left, has_right)
    right = ({"col": jnp.minimum(col + 1, cols - 1)}, has_right, has_left)

    barrier = pltpu.get_barrier_semaphore()
    for peer, there, _ in (up, down, left, right):

        @pl.when(there)
        def _():
            pl.semaphore_signal(barrier, inc=1, device_id=peer, device_id_type=MESH)

    arrays = (
        (p_hbm, pv), (a_hbm, av), (fine_columns_hbm, fine_columns), (fine_counts_hbm, fine_counts),
        (prolong_columns_hbm, prolong_columns), (prolong_counts_hbm, prolong_counts),
    )
    p_in, a_in, *codes_in = [
        pltpu.make_async_copy(src, dst, in_sem.at[at]) for at, (src, dst) in enumerate(arrays)
    ]
    for copy in (*codes_in, p_in, a_in):
        copy.start()

    class Remote:
        def __init__(self, number, src, dst, side):
            peer, self.sends, self.receives = side
            self.copy = pltpu.make_async_remote_copy(
                src_ref=src,
                dst_ref=dst,
                send_sem=send_sem.at[number],
                recv_sem=recv_sem.at[number],
                device_id=peer,
                device_id_type=MESH,
            )

        def start(self):
            pl.when(self.sends)(self.copy.start)

        def wait_send(self):
            pl.when(self.sends)(self.copy.wait_send)

        def wait_recv(self):
            pl.when(self.receives)(self.copy.wait_recv)

    remote = Remote

    for there, refs in (
        (has_up, (halo_t, got_u)),
        (has_down, (halo_b, got_d)),
        (has_left, (halo_l, corner_l, got_l)),
        (has_right, (halo_r, corner_r, got_r)),
    ):

        @pl.when(jnp.logical_not(there))
        def _():
            for ref in refs:
                ref[...] = jnp.zeros(ref.shape, ref.dtype)

    eye = (
        lax.broadcasted_iota(jnp.int32, (256, 256), 0)
        == lax.broadcasted_iota(jnp.int32, (256, 256), 1)
    ).astype(F32).astype(BF16)
    lane = lax.broadcasted_iota(jnp.int32, (1, 128), 1)
    line = lax.broadcasted_iota(jnp.int32, (16, 128), 0)
    half = lane < B

    def home_code(u, v, p):
        number = prolong_columns[u, v, p]
        code = (lax.bitwise_and(number, cols - 1) - col + 1) * 3 - row + 1
        code += lax.shift_right_logical(number, cols.bit_length() - 1)
        return jnp.where(p < prolong_counts[u, v], code, UNUSED)

    for copy in codes_in:
        copy.wait()
    codes = {(u, v): [home_code(u, v, p) for p in range(KP)] for u in range(AG) for v in range(AG)}

    def code_tile(ref, at, first, second):
        tile = jnp.zeros((16, 128), jnp.int32)
        for p in range(KP):
            tile = jnp.where(line == p, jnp.where(half, codes[first][p], codes[second][p]), tile)
        ref[KP * B :, at * 128 : (at + 1) * 128] = tile.astype(F32).astype(BF16)

    for u in range(AG):
        code_tile(ptx, 2 * u, (u, 0), (u, 1))
        code_tile(ptx, 2 * u + 1, (u, 2), (u, 3))
    for side, edge in ((0, edge_l), (AG - 1, edge_r)):
        code_tile(edge, 0, (0, side), (1, side))
        code_tile(edge, 1, (2, side), (3, side))
    p_in.wait()
    for side, edge in ((0, edge_l), (AG - 1, edge_r)):
        edge[0 : KP * B, :] = dot_nt(eye, pv[:, side].reshape(256, 256)).astype(BF16)
    for u in range(AG):
        ptx[0 : KP * B, u * 256 : (u + 1) * 256] = dot_nt(
            eye, pv[u].reshape(256, 256)
        ).astype(BF16)

    pl.semaphore_wait(barrier, sum(side[1].astype(jnp.int32) for side in (up, down, left, right)))
    to_up = remote(0, ptx.at[:, 0:256], halo_b, up)
    to_down = remote(1, ptx.at[:, 768:1024], halo_t, down)
    to_left = remote(2, edge_l, halo_r, left)
    to_right = remote(3, edge_r, halo_l, right)
    for copy in (to_up, to_down, to_left, to_right):
        copy.start()

    def own_dense(u, carry):
        lanes = pl.ds(pl.multiple_of(u * 256, 256), 256)
        dense(
            ptx, lanes, 256,
            lambda d, s: [
                (pdt, term_row(d, s), lanes),
                (r_own, window_row(d + 2, s + 1), lanes),
            ],
            blank_rows(r_own, lanes, (0, 4)),
        )
        return carry

    lax.fori_loop(0, AG, own_dense, 0)

    a_in.wait()
    tiles = ((1, 2), (3, 4), (0, 5))

    def toward_code(u, v, k):
        number = fine_columns[u, v, k]
        code = (lax.shift_right_logical(number, fine_cols.bit_length() - 1) - row * AG - u) * 3
        code += lax.bitwise_and(number, fine_cols - 1) - col * AG - v + 4
        return jnp.where(k < fine_counts[u, v], code, UNUSED)

    def strip(u, carry):
        for v in range(AG):
            wide = [av[u, v, :, 128 * t : 128 * (t + 1)] for t in range(4)]
            last = av[u, v, :, 512:576]
            wide.append(jnp.concatenate([last, jnp.zeros_like(last)], axis=1))
            wide = wide + [swapped(w).astype(BF16) for w in wide]
            wide = [w.reshape(4, 16, 128) for w in wide]
            codes = jnp.full((16, 128), UNUSED, jnp.int32)
            toward = [toward_code(u, v, k) for k in range(KA)] + [UNUSED]
            for t in range(5):
                one, two = toward[2 * t], toward[2 * t + 1]
                codes = jnp.where(line == t, jnp.where(half, one, two), codes)
                codes = jnp.where(line == t + 5, jnp.where(half, two, one), codes)
            for at, pair in enumerate(tiles):
                sides = [target - 1 - v for target in pair]
                for dr in (-1, 0, 1):
                    here = (u + dr + 1, pl.ds((1 - dr) * 256 + v * B, B), pl.ds(at * 128, 128))
                    wanted = [(dr + 1) * 3 + dc + 1 if abs(dc) <= 1 else 99 for dc in sides]
                    if wanted == [99, 99]:
                        aw[here] = jnp.zeros((B, 128), BF16)
                        continue
                    match = jnp.where(
                        codes == jnp.where(half, wanted[0], wanted[1]), 1.0, 0.0
                    )
                    total = None
                    for t in range(10):
                        if wanted[0] == 99 and t == 4 or wanted[1] == 99 and t == 9:
                            continue
                        mask = jnp.broadcast_to(match[t : t + 1], (16, 128)).astype(BF16)
                        part = mask[None] * wide[t]
                        total = part if total is None else total + part
                    aw[here] = total.reshape(B, 128)
        return carry

    lax.fori_loop(0, AG, strip, 0)

    def row_of_targets(w):
        first, last = max(w - 1, 0), min(w + 1, AG - 1)
        got = dot_nn(
            pdt[:, first * 256 : (last + 1) * 256],
            aw[w + 1, (first - w + 1) * 256 : (last - w + 2) * 256, :],
        )
        place = w if 0 <= w < AG else (AG if w < 0 else AG + 1)
        q_own[:, place * 256 : (place + 1) * 256] = got[:, 0:256].astype(BF16)
        return got[:, 256:384]

    for at, (w0, w1) in enumerate(((0, 1), (2, 3), (-1, 4))):
        x, y = row_of_targets(w0), row_of_targets(w1)
        lanes = slice(at * 128, (at + 1) * 128)
        q_l[:, lanes] = jnp.where(half, x, pltpu.roll(y, B, 1)).astype(BF16)
        q_r[:, lanes] = jnp.where(half, pltpu.roll(x, B, 1), y).astype(BF16)

    c_side[:, 0:256] = jnp.zeros((384, 256), F32)
    c_side[:, 1280:WIDE] = jnp.zeros((384, WIDE - 1280), F32)
    c_mid[:, 0:384] = jnp.zeros((192, 384), F32)
    c_mid[:, 1408:WIDE] = jnp.zeros((192, WIDE - 1408), F32)
    c_side[:, 256:1280] = dot_nt(q_own[0:384, 0:1024], r_own[0:1024, 0:1024])
    c_mid[:, 384:1408] = dot_nt(q_own[384:576, 0:1024], r_own[64:1088, 0:1024])

    to_down.wait_recv()
    to_up.wait_recv()
    for rows_16 in range(PT_ROWS // 16):
        at = slice(rows_16 * 16, (rows_16 + 1) * 16)
        pass_l[at, :] = jnp.where(
            half, halo_t[at, 0:128].astype(F32), swapped(halo_b[at, 0:128])
        ).astype(BF16)
        pass_r[at, :] = jnp.where(
            half, swapped(halo_t[at, 128:256]), halo_b[at, 128:256].astype(F32)
        ).astype(BF16)
    corner_to_left = remote(4, pass_l, corner_r, left)
    corner_to_right = remote(5, pass_r, corner_l, right)
    corner_to_left.start()
    corner_to_right.start()

    for halo, shift, blanks, first in ((halo_t, 1, (3, 4), 1024), (halo_b, 3, (0, 1), 1280)):
        at = slice(first, first + 256)
        dense(
            halo, slice(0, 256), 256,
            lambda d, s: [(r_own, window_row(d + shift, s + 1), at)],
            blank_rows(r_own, at, blanks),
        )
    to_left.wait_recv()
    to_right.wait_recv()
    for halo, ref in ((halo_l, r_l), (halo_r, r_r)):
        at = slice(0, 256)
        dense(
            halo, at, 256,
            lambda d, s: [(ref, window_row(d + 2, s + 1), at)],
            blank_rows(ref, at, (0, 4)),
        )
    c_side[:, 256:1280] += dot_nt(q_own[0:384, 1024:1536], r_own[0:1024, 1024:1536])

    corner_to_left.wait_recv()
    corner_to_right.wait_recv()
    for corner, ref in ((corner_l, r_l), (corner_r, r_r)):
        spread, blocks = slot_parts(corner, slice(0, 128), 128)
        for side in (-1, 0, 1):
            for j in range(5):
                above, below = j - 1, j - 3
                codes = [home(d, side) if abs(d) <= 1 else 99 for d in (above, below)]
                code = jnp.where(half, codes[0], codes[1]).astype(F32).astype(BF16)
                row_at = window_row(j, side + 1)
                ref[row_at : row_at + B, 256:384] = chosen(spread, blocks, range(KP), code)
        for row_at in (0, 16 * B):
            ref[row_at : row_at + B, 256:384] = jnp.zeros((B, 128), BF16)
    c_side[:, 0:1024] += dot_nt(q_l[0:384, :], r_l[64:1088, :])
    c_side[:, 640:WIDE] += dot_nt(q_r[0:384, :], r_r[64:1088, :])

    send_l[...] = c_side[0:192, :].astype(BF16)
    send_r[...] = c_side[192:384, :].astype(BF16)
    side_copies = []
    for number, at in ((6, slice(0, 128)), (8, slice(128, 192))):
        to_l = remote(number, send_l.at[at], got_r.at[at], left)
        to_r = remote(number + 1, send_r.at[at], got_l.at[at], right)
        to_l.start()
        to_r.start()
        side_copies.append((to_l, to_r))

    c_mid[:, 384:1408] += dot_nt(q_own[384:576, 1024:1536], r_own[64:1088, 1024:1536])
    c_mid[:, 0:1024] += dot_nt(q_l[384:576, :], r_l[0:1024, :])
    c_mid[:, 640:WIDE] += dot_nt(q_r[384:576, :], r_r[0:1024, :])

    def folded(at, lo, hi):
        total = None
        for ref, first in ((got_l, 0), (c_mid, 256), (got_r, 640)):
            if first <= lo and hi <= first + WIDE:
                part = ref[at, lo - first : hi - first].astype(F32)
                total = part if total is None else total + part
        return total

    spans = ((0, 256), (256, 640), (640, 1664), (1664, 1920), (1920, FULL))
    for copy in side_copies[0]:
        copy.wait_recv()
    for lo, hi in spans:
        send_rows[:, lo:hi] = folded(slice(0, 128), lo, hi).astype(BF16)
    to_u = remote(10, send_rows.at[0:64], got_d, up)
    to_d = remote(11, send_rows.at[64:128], got_u, down)
    to_u.start()
    to_d.start()
    for copy in side_copies[1]:
        copy.wait_recv()
    for lo, hi in spans:
        e_mid[:, lo:hi] = folded(slice(128, 192), lo, hi)
    to_u.wait_recv()
    to_d.wait_recv()

    for s in range(7):
        for t in range(7):
            total = None
            for ref, j in ((got_u, s), (e_mid, s - 1), (got_d, s - 2)):
                if 0 <= j < 5:
                    at = (t * 5 + j) * B
                    part = ref[:, at : at + B].astype(F32)
                    total = part if total is None else total + part
            at = (s * 7 + t) * B
            out_ref[0, 0, :, at : at + B] = total.astype(BF16)

    sent = [to_up, to_down, to_left, to_right, corner_to_left, corner_to_right, to_u, to_d]
    for copy in sent + [copy for pair in side_copies for copy in pair]:
        copy.wait_send()


def per_device(
    fine_blocks, fine_columns, fine_counts, prolong_blocks, prolong_columns, prolong_counts
):
    vmem = pl.BlockSpec(memory_space=pltpu.VMEM)
    hbm = pl.BlockSpec(memory_space=pltpu.HBM)
    return pl.pallas_call(
        kernel,
        out_shape=jax.ShapeDtypeStruct((1, 1, B, 49 * B), BF16),
        in_specs=[hbm] * 6,
        out_specs=vmem,
        scratch_shapes=[
            pltpu.SMEM((AG, AG, KA), jnp.int32),
            pltpu.SMEM((AG, AG), jnp.int32),
            pltpu.SMEM((AG, AG, KP), jnp.int32),
            pltpu.SMEM((AG, AG), jnp.int32),
            pltpu.VMEM((AG, AG, B, KP * B), BF16),
            pltpu.VMEM((AG, AG, B, KA * B), BF16),
            pltpu.VMEM((PT_ROWS, 1024), BF16),
            pltpu.VMEM((PT_ROWS, 256), BF16),
            pltpu.VMEM((PT_ROWS, 256), BF16),
            pltpu.VMEM((PT_ROWS, 256), BF16),
            pltpu.VMEM((PT_ROWS, 256), BF16),
            pltpu.VMEM((PT_ROWS, 256), BF16),
            pltpu.VMEM((PT_ROWS, 256), BF16),
            pltpu.VMEM((PT_ROWS, 128), BF16),
            pltpu.VMEM((PT_ROWS, 128), BF16),
            pltpu.VMEM((PT_ROWS, 128), BF16),
            pltpu.VMEM((PT_ROWS, 128), BF16),
            pltpu.VMEM((9 * B, 1024), BF16),
            pltpu.VMEM((6, 768, 384), BF16),
            pltpu.VMEM((9 * B, 1536), BF16),
            pltpu.VMEM((9 * B, 384), BF16),
            pltpu.VMEM((9 * B, 384), BF16),
            pltpu.VMEM((R_ROWS, 1536), BF16),
            pltpu.VMEM((R_ROWS, 384), BF16),
            pltpu.VMEM((R_ROWS, 384), BF16),
            pltpu.VMEM((6 * B, WIDE), F32),
            pltpu.VMEM((3 * B, WIDE), F32),
            pltpu.VMEM((3 * B, WIDE), BF16),
            pltpu.VMEM((3 * B, WIDE), BF16),
            pltpu.VMEM((3 * B, WIDE), BF16),
            pltpu.VMEM((3 * B, WIDE), BF16),
            pltpu.VMEM((2 * B, FULL), BF16),
            pltpu.VMEM((B, FULL), F32),
            pltpu.VMEM((B, FULL), BF16),
            pltpu.VMEM((B, FULL), BF16),
            pltpu.SemaphoreType.DMA((6,)),
            pltpu.SemaphoreType.DMA((12,)),
            pltpu.SemaphoreType.DMA((12,)),
        ],
        compiler_params=pltpu.CompilerParams(
            collective_id=0, has_side_effects=True, vmem_limit_bytes=62 * 2**20
        ),
    )(
        prolong_blocks, fine_blocks,
        fine_columns, fine_counts, prolong_columns, prolong_counts,
    )


def solution(mesh):
    in_specs = (
        P("row", "col", None, None),
        P("row", "col", None),
        P("row", "col"),
        P("row", "col", None, None),
        P("row", "col", None),
        P("row", "col"),
    )
    return jax.shard_map(
        per_device,
        mesh=mesh,
        in_specs=in_specs,
        out_specs=P("row", "col", None, None),
        check_vma=False,
    )
```

```python
import functools

import jax
import jax.numpy as jnp
from jax import lax
from jax.experimental import pallas as pl
from jax.experimental.pallas import tpu as pltpu
from jax.sharding import PartitionSpec as P

MESH = pl.DeviceIdType.MESH
F32 = jnp.float32
BF16 = jnp.bfloat16

B = 64
KA = 9
KP = 4
AG = 4
UNUSED = 15
PT_ROWS = KP * B + 16
ORDER = {-1: 0, 1: 1, 0: 2}
WIDE = 26 * B
FULL = 36 * B
CHUNKS = 4
R_ROWS = 17 * B


def dot_nn(a, b):
    return lax.dot_general(a, b, (((1,), (0,)), ((), ())), preferred_element_type=F32)


def dot_nt(a, b):
    return lax.dot_general(a, b, (((1,), (1,)), ((), ())), preferred_element_type=F32)


def term_row(down, side):
    return (ORDER[side] * 3 + ORDER[down]) * B


def home(down, side):
    return (side + 1) * 3 + down + 1


def window_row(down, side):
    return (1 + side * 5 + down) * B


def swapped(x):
    return pltpu.roll(x.astype(F32), B, 1)


def slot_parts(x_ref, lanes, width):
    codes = x_ref[KP * B : PT_ROWS, lanes].astype(F32)
    spread = [
        jnp.broadcast_to(codes[p : p + 1], (16, width)).astype(BF16) for p in range(KP)
    ]
    blocks = [x_ref[p * B : (p + 1) * B, lanes].reshape(4, 16, width) for p in range(KP)]
    return spread, blocks


def chosen(spread, blocks, slots, code):
    total = None
    for p in slots:
        part = jnp.where((spread[p] == code)[None], blocks[p], jnp.zeros_like(blocks[p]))
        total = part if total is None else total + part
    return total.reshape(B, total.shape[-1])


def dense(x_ref, lanes, width, places, zeros):
    spread, blocks = slot_parts(x_ref, lanes, width)
    for down in (-1, 0, 1):
        for side in (-1, 0, 1):
            code = home(down, side)
            slots = range(KP) if code == 4 else range(1, KP)
            value = chosen(spread, blocks, slots, jnp.array(code, BF16))
            for ref, row, at in places(down, side):
                ref[row : row + B, at] = value
    for ref, row, at in zeros:
        ref[row : row + B, at] = jnp.zeros((B, width), BF16)


def blank_rows(ref, at, downs):
    rows = [0, 16 * B] + [window_row(d, s) for s in range(3) for d in downs]
    return [(ref, row, at) for row in rows]


def kernel(
    p_hbm, a_hbm, fine_columns_hbm, fine_counts_hbm, prolong_columns_hbm, prolong_counts_hbm, out_ref,
    fine_columns, fine_counts, prolong_columns, prolong_counts,
    pv, av, ptx, edge_l, edge_r, halo_t, halo_b, halo_l, halo_r,
    pack_tl, pack_tr, pack_bl, pack_br, land_tl, land_tr, land_bl, land_br, corner_l, corner_r,
    pdt, aw, q_own, q_l, q_r, r_own, r_l, r_r, c_side, c_mid,
    send_l, send_r, got_l, got_r, send_rows, e_mid, got_u, got_d,
    in_sem, send_sem, recv_sem,
):
    row, col = lax.axis_index("row"), lax.axis_index("col")
    rows, cols = lax.axis_size("row"), lax.axis_size("col")
    fine_cols = AG * cols
    def there(d, s):
        r, c = row + d, col + s
        return jnp.logical_and(jnp.logical_and(r >= 0, r < rows), jnp.logical_and(c >= 0, c < cols))

    def side(d, s):
        peer = {"row": jnp.clip(row + d, 0, rows - 1), "col": jnp.clip(col + s, 0, cols - 1)}
        return peer, there(d, s), there(-d, -s)

    up, down, left, right = side(-1, 0), side(1, 0), side(0, -1), side(0, 1)
    up_left, up_right, down_left, down_right = side(-1, -1), side(-1, 1), side(1, -1), side(1, 1)
    sides = (up, down, left, right, up_left, up_right, down_left, down_right)

    barrier = pltpu.get_barrier_semaphore()
    for peer, present, _ in sides:

        @pl.when(present)
        def _():
            pl.semaphore_signal(barrier, inc=1, device_id=peer, device_id_type=MESH)

    arrays = (
        (p_hbm, pv), (a_hbm, av), (fine_columns_hbm, fine_columns), (fine_counts_hbm, fine_counts),
        (prolong_columns_hbm, prolong_columns), (prolong_counts_hbm, prolong_counts),
    )
    p_in, a_in, *codes_in = [
        pltpu.make_async_copy(src, dst, in_sem.at[at]) for at, (src, dst) in enumerate(arrays)
    ]
    for copy in (*codes_in, p_in, a_in):
        copy.start()

    class Remote:
        def __init__(self, number, src, dst, side):
            peer, self.sends, self.receives = side
            self.copy = pltpu.make_async_remote_copy(
                src_ref=src,
                dst_ref=dst,
                send_sem=send_sem.at[number],
                recv_sem=recv_sem.at[number],
                device_id=peer,
                device_id_type=MESH,
            )

        def start(self):
            pl.when(self.sends)(self.copy.start)

        def wait_send(self):
            pl.when(self.sends)(self.copy.wait_send)

        def wait_recv(self):
            pl.when(self.receives)(self.copy.wait_recv)

    remote = Remote

    for (_, present, _), refs in (
        (up, (halo_t, got_u)),
        (down, (halo_b, got_d)),
        (left, (halo_l, got_l)),
        (right, (halo_r, got_r)),
        (up_left, (land_tl,)),
        (up_right, (land_tr,)),
        (down_left, (land_bl,)),
        (down_right, (land_br,)),
    ):

        @pl.when(jnp.logical_not(present))
        def _():
            for ref in refs:
                ref[...] = jnp.zeros(ref.shape, ref.dtype)

    eye = (
        lax.broadcasted_iota(jnp.int32, (256, 256), 0)
        == lax.broadcasted_iota(jnp.int32, (256, 256), 1)
    ).astype(F32).astype(BF16)
    lane = lax.broadcasted_iota(jnp.int32, (1, 128), 1)
    line = lax.broadcasted_iota(jnp.int32, (16, 128), 0)
    half = lane < B

    def home_code(u, v, p):
        number = prolong_columns[u, v, p]
        code = (lax.bitwise_and(number, cols - 1) - col + 1) * 3 - row + 1
        code += lax.shift_right_logical(number, cols.bit_length() - 1)
        return jnp.where(p < prolong_counts[u, v], code, UNUSED)

    for copy in codes_in:
        copy.wait()
    codes = {(u, v): [home_code(u, v, p) for p in range(KP)] for u in range(AG) for v in range(AG)}

    def code_tile(ref, at, first, second):
        tile = jnp.zeros((16, 128), jnp.int32)
        for p in range(KP):
            tile = jnp.where(line == p, jnp.where(half, codes[first][p], codes[second][p]), tile)
        ref[KP * B :, at * 128 : (at + 1) * 128] = tile.astype(F32).astype(BF16)

    for u in range(AG):
        code_tile(ptx, 2 * u, (u, 0), (u, 1))
        code_tile(ptx, 2 * u + 1, (u, 2), (u, 3))
    for side, edge in ((0, edge_l), (AG - 1, edge_r)):
        code_tile(edge, 0, (0, side), (1, side))
        code_tile(edge, 1, (2, side), (3, side))
    p_in.wait()
    for side, edge in ((0, edge_l), (AG - 1, edge_r)):
        edge[0 : KP * B, :] = dot_nt(eye, pv[:, side].reshape(256, 256)).astype(BF16)
    for u in range(AG):
        ptx[0 : KP * B, u * 256 : (u + 1) * 256] = dot_nt(
            eye, pv[u].reshape(256, 256)
        ).astype(BF16)

    low, high, last = slice(0, 2 * B), slice(2 * B, 4 * B), slice(KP * B, PT_ROWS)
    for pack, at, in_right, is_top in (
        (pack_tl, 0, False, False),
        (pack_tr, 1, True, False),
        (pack_bl, 6, False, True),
        (pack_br, 7, True, True),
    ):
        tile = slice(at * 128, (at + 1) * 128)
        first, second = (low, high) if is_top else (high, low)
        one, two = ptx[first, tile].astype(F32), ptx[second, tile].astype(F32)
        if in_right:
            one = pltpu.roll(one, B, 1)
        else:
            two = pltpu.roll(two, B, 1)
        pack[0 : 2 * B, :] = jnp.where(half, one, two).astype(BF16)
        code = ptx[last, tile].astype(F32)
        pack[2 * B :, :] = (pltpu.roll(code, B, 1) if in_right == is_top else code).astype(BF16)

    pl.semaphore_wait(barrier, sum(present.astype(jnp.int32) for _, present, _ in sides))
    to_up = remote(0, ptx.at[:, 0:256], halo_b, up)
    to_down = remote(1, ptx.at[:, 768:1024], halo_t, down)
    to_left = remote(2, edge_l, halo_r, left)
    to_right = remote(3, edge_r, halo_l, right)
    corners_out = (
        remote(4, pack_tl, land_br, up_left),
        remote(5, pack_tr, land_bl, up_right),
        remote(24, pack_bl, land_tr, down_left),
        remote(25, pack_br, land_tl, down_right),
    )
    halo_out = (to_up, to_down, to_left, to_right, *corners_out)
    for copy in halo_out:
        copy.start()

    def own_dense(u, carry):
        lanes = pl.ds(pl.multiple_of(u * 256, 256), 256)
        dense(
            ptx, lanes, 256,
            lambda d, s: [
                (pdt, term_row(d, s), lanes),
                (r_own, window_row(d + 2, s + 1), lanes),
            ],
            blank_rows(r_own, lanes, (0, 4)),
        )
        return carry

    lax.fori_loop(0, AG, own_dense, 0)

    a_in.wait()
    tiles = ((1, 2), (3, 4), (0, 5))

    def toward_code(u, v, k):
        number = fine_columns[u, v, k]
        code = (lax.shift_right_logical(number, fine_cols.bit_length() - 1) - row * AG - u) * 3
        code += lax.bitwise_and(number, fine_cols - 1) - col * AG - v + 4
        return jnp.where(k < fine_counts[u, v], code, UNUSED)

    def strip(u, carry):
        for v in range(AG):
            wide = [av[u, v, :, 128 * t : 128 * (t + 1)] for t in range(4)]
            last = av[u, v, :, 512:576]
            wide.append(jnp.concatenate([last, jnp.zeros_like(last)], axis=1))
            wide = wide + [swapped(w).astype(BF16) for w in wide]
            wide = [w.reshape(4, 16, 128) for w in wide]
            codes = jnp.full((16, 128), UNUSED, jnp.int32)
            toward = [toward_code(u, v, k) for k in range(KA)] + [UNUSED]
            for t in range(5):
                one, two = toward[2 * t], toward[2 * t + 1]
                codes = jnp.where(line == t, jnp.where(half, one, two), codes)
                codes = jnp.where(line == t + 5, jnp.where(half, two, one), codes)
            for at, pair in enumerate(tiles):
                sides = [target - 1 - v for target in pair]
                for dr in (-1, 0, 1):
                    here = (u + dr + 1, pl.ds((1 - dr) * 256 + v * B, B), pl.ds(at * 128, 128))
                    wanted = [(dr + 1) * 3 + dc + 1 if abs(dc) <= 1 else 99 for dc in sides]
                    if wanted == [99, 99]:
                        aw[here] = jnp.zeros((B, 128), BF16)
                        continue
                    match = jnp.where(
                        codes == jnp.where(half, wanted[0], wanted[1]), 1.0, 0.0
                    )
                    total = None
                    for t in range(10):
                        if wanted[0] == 99 and t == 4 or wanted[1] == 99 and t == 9:
                            continue
                        mask = jnp.broadcast_to(match[t : t + 1], (16, 128)).astype(BF16)
                        part = mask[None] * wide[t]
                        total = part if total is None else total + part
                    aw[here] = total.reshape(B, 128)
        return carry

    lax.fori_loop(0, AG, strip, 0)

    def row_of_targets(w):
        first, last = max(w - 1, 0), min(w + 1, AG - 1)
        got = dot_nn(
            pdt[:, first * 256 : (last + 1) * 256],
            aw[w + 1, (first - w + 1) * 256 : (last - w + 2) * 256, :],
        )
        place = w if 0 <= w < AG else (AG if w < 0 else AG + 1)
        q_own[:, place * 256 : (place + 1) * 256] = got[:, 0:256].astype(BF16)
        return got[:, 256:384]

    for at, (w0, w1) in enumerate(((0, 1), (2, 3), (-1, 4))):
        x, y = row_of_targets(w0), row_of_targets(w1)
        lanes = slice(at * 128, (at + 1) * 128)
        q_l[:, lanes] = jnp.where(half, x, pltpu.roll(y, B, 1)).astype(BF16)
        q_r[:, lanes] = jnp.where(half, pltpu.roll(x, B, 1), y).astype(BF16)

    c_side[:, 0:256] = jnp.zeros((384, 256), F32)
    c_side[:, 1280:WIDE] = jnp.zeros((384, WIDE - 1280), F32)
    c_mid[:, 0:384] = jnp.zeros((192, 384), F32)
    c_mid[:, 1408:WIDE] = jnp.zeros((192, WIDE - 1408), F32)
    c_side[:, 256:1280] = dot_nt(q_own[0:384, 0:1024], r_own[0:1024, 0:1024])
    c_mid[:, 384:1408] = dot_nt(q_own[384:576, 0:1024], r_own[64:1088, 0:1024])

    to_down.wait_recv()
    to_up.wait_recv()
    for halo, shift, blanks, first in ((halo_t, 1, (3, 4), 1024), (halo_b, 3, (0, 1), 1280)):
        at = slice(first, first + 256)
        dense(
            halo, slice(0, 256), 256,
            lambda d, s: [(r_own, window_row(d + shift, s + 1), at)],
            blank_rows(r_own, at, blanks),
        )
    to_left.wait_recv()
    to_right.wait_recv()
    for halo, ref in ((halo_l, r_l), (halo_r, r_r)):
        at = slice(0, 256)
        dense(
            halo, at, 256,
            lambda d, s: [(ref, window_row(d + 2, s + 1), at)],
            blank_rows(ref, at, (0, 4)),
        )
    c_side[:, 256:1280] += dot_nt(q_own[0:384, 1024:1536], r_own[0:1024, 1024:1536])

    for copy in corners_out:
        copy.wait_recv()
    for top, bottom, corner in ((land_tl, land_bl, corner_l), (land_tr, land_br, corner_r)):
        one, two = top[0 : 2 * B, :], bottom[0 : 2 * B, :]
        corner[low, :] = jnp.where(half, one, two)
        corner[high, :] = swapped(jnp.where(half, two, one)).astype(BF16)
        corner[last, :] = jnp.where(half, top[2 * B :, :], bottom[2 * B :, :])
    for corner, ref in ((corner_l, r_l), (corner_r, r_r)):
        spread, blocks = slot_parts(corner, slice(0, 128), 128)
        for side in (-1, 0, 1):
            for j in range(5):
                above, below = j - 1, j - 3
                codes = [home(d, side) if abs(d) <= 1 else 99 for d in (above, below)]
                code = jnp.where(half, codes[0], codes[1]).astype(F32).astype(BF16)
                row_at = window_row(j, side + 1)
                ref[row_at : row_at + B, 256:384] = chosen(spread, blocks, range(KP), code)
        for row_at in (0, 16 * B):
            ref[row_at : row_at + B, 256:384] = jnp.zeros((B, 128), BF16)
    c_side[:, 0:1024] += dot_nt(q_l[0:384, :], r_l[64:1088, :])
    c_side[:, 640:WIDE] += dot_nt(q_r[0:384, :], r_r[64:1088, :])

    side_copies = []
    for q in range(CHUNKS):
        for h in range(2):
            at, first = slice(q * 32 + h * 16, q * 32 + h * 16 + 16), h * B + q * 16
            send_l[at, :] = c_side[first : first + 16, :].astype(BF16)
            send_r[at, :] = c_side[192 + first : 208 + first, :].astype(BF16)
        at = slice(q * 32, q * 32 + 32)
        pair = (
            remote(6 + 2 * q, send_l.at[at], got_r.at[at], left),
            remote(7 + 2 * q, send_r.at[at], got_l.at[at], right),
        )
        for copy in pair:
            copy.start()
        side_copies.append(pair)
    send_l[128:192, :] = c_side[128:192, :].astype(BF16)
    send_r[128:192, :] = c_side[320:384, :].astype(BF16)

    c_mid[:, 384:1408] += dot_nt(q_own[384:576, 1024:1536], r_own[64:1088, 1024:1536])
    c_mid[:, 0:1024] += dot_nt(q_l[384:576, :], r_l[0:1024, :])
    c_mid[:, 640:WIDE] += dot_nt(q_r[384:576, :], r_r[0:1024, :])

    def folded(got_at, mid_at, lo, hi):
        total = None
        for ref, at, first in ((got_l, got_at, 0), (c_mid, mid_at, 256), (got_r, got_at, 640)):
            if first <= lo and hi <= first + WIDE:
                part = ref[at, lo - first : hi - first].astype(F32)
                total = part if total is None else total + part
        return total

    spans = ((0, 256), (256, 640), (640, 1664), (1664, 1920), (1920, FULL))
    row_copies = []
    for q in range(CHUNKS):
        for copy in side_copies[q]:
            copy.wait_recv()
        for h in range(2):
            at, first = slice(q * 32 + h * 16, q * 32 + h * 16 + 16), h * B + q * 16
            for lo, hi in spans:
                send_rows[at, lo:hi] = folded(at, slice(first, first + 16), lo, hi).astype(BF16)
        at = slice(q * 16, q * 16 + 16)
        pair = (
            remote(16 + 2 * q, send_rows.at[q * 32 : q * 32 + 16], got_d.at[at], up),
            remote(17 + 2 * q, send_rows.at[q * 32 + 16 : q * 32 + 32], got_u.at[at], down),
        )
        for copy in pair:
            copy.start()
        row_copies.append(pair)
    at = slice(128, 192)
    side_copies.append(
        (
            remote(14, send_l.at[at], got_r.at[at], left),
            remote(15, send_r.at[at], got_l.at[at], right),
        )
    )
    for copy in side_copies[CHUNKS]:
        copy.start()
    for copy in side_copies[CHUNKS]:
        copy.wait_recv()
    for lo, hi in spans:
        e_mid[:, lo:hi] = folded(at, at, lo, hi)

    for q in range(CHUNKS):
        for copy in row_copies[q]:
            copy.wait_recv()
        rows_16 = slice(q * 16, q * 16 + 16)
        for s in range(7):
            for t in range(7):
                total = None
                for ref, j in ((got_u, s), (e_mid, s - 1), (got_d, s - 2)):
                    if 0 <= j < 5:
                        at = (t * 5 + j) * B
                        part = ref[rows_16, at : at + B].astype(F32)
                        total = part if total is None else total + part
                at = (s * 7 + t) * B
                out_ref[0, 0, rows_16, at : at + B] = total.astype(BF16)

    for copy in [*halo_out] + [copy for pair in side_copies + row_copies for copy in pair]:
        copy.wait_send()


def per_device(
    fine_blocks, fine_columns, fine_counts, prolong_blocks, prolong_columns, prolong_counts
):
    vmem = pl.BlockSpec(memory_space=pltpu.VMEM)
    hbm = pl.BlockSpec(memory_space=pltpu.HBM)
    return pl.pallas_call(
        kernel,
        out_shape=jax.ShapeDtypeStruct((1, 1, B, 49 * B), BF16),
        in_specs=[hbm] * 6,
        out_specs=vmem,
        scratch_shapes=[
            pltpu.SMEM((AG, AG, KA), jnp.int32),
            pltpu.SMEM((AG, AG), jnp.int32),
            pltpu.SMEM((AG, AG, KP), jnp.int32),
            pltpu.SMEM((AG, AG), jnp.int32),
            pltpu.VMEM((AG, AG, B, KP * B), BF16),
            pltpu.VMEM((AG, AG, B, KA * B), BF16),
            pltpu.VMEM((PT_ROWS, 1024), BF16),
            pltpu.VMEM((PT_ROWS, 256), BF16),
            pltpu.VMEM((PT_ROWS, 256), BF16),
            pltpu.VMEM((PT_ROWS, 256), BF16),
            pltpu.VMEM((PT_ROWS, 256), BF16),
            pltpu.VMEM((PT_ROWS, 256), BF16),
            pltpu.VMEM((PT_ROWS, 256), BF16),
            *[pltpu.VMEM((2 * B + 16, 128), BF16)] * 8,
            pltpu.VMEM((PT_ROWS, 128), BF16),
            pltpu.VMEM((PT_ROWS, 128), BF16),
            pltpu.VMEM((9 * B, 1024), BF16),
            pltpu.VMEM((6, 768, 384), BF16),
            pltpu.VMEM((9 * B, 1536), BF16),
            pltpu.VMEM((9 * B, 384), BF16),
            pltpu.VMEM((9 * B, 384), BF16),
            pltpu.VMEM((R_ROWS, 1536), BF16),
            pltpu.VMEM((R_ROWS, 384), BF16),
            pltpu.VMEM((R_ROWS, 384), BF16),
            pltpu.VMEM((6 * B, WIDE), F32),
            pltpu.VMEM((3 * B, WIDE), F32),
            pltpu.VMEM((3 * B, WIDE), BF16),
            pltpu.VMEM((3 * B, WIDE), BF16),
            pltpu.VMEM((3 * B, WIDE), BF16),
            pltpu.VMEM((3 * B, WIDE), BF16),
            pltpu.VMEM((2 * B, FULL), BF16),
            pltpu.VMEM((B, FULL), F32),
            pltpu.VMEM((B, FULL), BF16),
            pltpu.VMEM((B, FULL), BF16),
            pltpu.SemaphoreType.DMA((6,)),
            pltpu.SemaphoreType.DMA((26,)),
            pltpu.SemaphoreType.DMA((26,)),
        ],
        compiler_params=pltpu.CompilerParams(
            collective_id=0, has_side_effects=True, vmem_limit_bytes=62 * 2**20
        ),
    )(
        prolong_blocks, fine_blocks,
        fine_columns, fine_counts, prolong_columns, prolong_counts,
    )


def solution(mesh):
    in_specs = (
        P("row", "col", None, None),
        P("row", "col", None),
        P("row", "col"),
        P("row", "col", None, None),
        P("row", "col", None),
        P("row", "col"),
    )
    return jax.shard_map(
        per_device,
        mesh=mesh,
        in_specs=in_specs,
        out_specs=P("row", "col", None, None),
        check_vma=False,
    )
```

```python
import functools

import jax
import jax.numpy as jnp
from jax import lax
from jax.experimental import pallas as pl
from jax.experimental.pallas import tpu as pltpu
from jax.sharding import PartitionSpec as P

MESH = pl.DeviceIdType.MESH
F32 = jnp.float32
BF16 = jnp.bfloat16

B = 64
KA = 9
KP = 4
AG = 4
UNUSED = 15
PT_ROWS = KP * B + 16
ORDER = {-1: 0, 1: 1, 0: 2}
WIDE = 26 * B
FULL = 36 * B
CHUNKS = 4
PLACES = (0, 3, 1, 2)
R_ROWS = 17 * B


def dot_nn(a, b):
    return lax.dot_general(a, b, (((1,), (0,)), ((), ())), preferred_element_type=F32)


def dot_nt(a, b):
    return lax.dot_general(a, b, (((1,), (1,)), ((), ())), preferred_element_type=F32)


def term_row(down, side):
    return (ORDER[side] * 3 + ORDER[down]) * B


def home(down, side):
    return (side + 1) * 3 + down + 1


def window_row(down, side):
    return (1 + side * 5 + down) * B


def swapped(x):
    return pltpu.roll(x.astype(F32), B, 1)


def slot_parts(x_ref, lanes, width):
    codes = x_ref[KP * B : PT_ROWS, lanes].astype(F32)
    spread = [
        jnp.broadcast_to(codes[p : p + 1], (16, width)).astype(BF16) for p in range(KP)
    ]
    blocks = [x_ref[p * B : (p + 1) * B, lanes].reshape(4, 16, width) for p in range(KP)]
    return spread, blocks


def chosen(spread, blocks, slots, code):
    total = None
    for p in slots:
        part = jnp.where((spread[p] == code)[None], blocks[p], jnp.zeros_like(blocks[p]))
        total = part if total is None else total + part
    return total.reshape(B, total.shape[-1])


def dense(x_ref, lanes, width, places, zeros):
    spread, blocks = slot_parts(x_ref, lanes, width)
    for down in (-1, 0, 1):
        for side in (-1, 0, 1):
            code = home(down, side)
            slots = range(KP) if code == 4 else range(1, KP)
            value = chosen(spread, blocks, slots, jnp.array(code, BF16))
            for ref, row, at in places(down, side):
                ref[row : row + B, at] = value
    for ref, row, at in zeros:
        ref[row : row + B, at] = jnp.zeros((B, width), BF16)


def blank_rows(ref, at, downs):
    rows = [0, 16 * B] + [window_row(d, s) for s in range(3) for d in downs]
    return [(ref, row, at) for row in rows]


def kernel(
    p_hbm, a_hbm, fine_columns_hbm, fine_counts_hbm, prolong_columns_hbm, prolong_counts_hbm, out_ref,
    fine_columns, fine_counts, prolong_columns, prolong_counts,
    pv, av, ptx, edge_l, edge_r, halo_t, halo_b, halo_l, halo_r,
    pass_l, pass_r, corner_l, corner_r,
    pdt, pdt_l, pdt_r, aw, aw_l, aw_r, q_own, q_l, q_r, r_own, r_l, r_r, c_side, c_mid,
    send_l, send_r, got_l, got_r, send_rows, e_mid, got_u, got_d,
    in_sem, send_sem, recv_sem,
):
    row, col = lax.axis_index("row"), lax.axis_index("col")
    rows, cols = lax.axis_size("row"), lax.axis_size("col")
    fine_cols = AG * cols
    def there(d, s):
        r, c = row + d, col + s
        return jnp.logical_and(jnp.logical_and(r >= 0, r < rows), jnp.logical_and(c >= 0, c < cols))

    def side(d, s):
        peer = {"row": jnp.clip(row + d, 0, rows - 1), "col": jnp.clip(col + s, 0, cols - 1)}
        return peer, there(d, s), there(-d, -s)

    up, down, left, right = side(-1, 0), side(1, 0), side(0, -1), side(0, 1)
    sides = (up, down, left, right)

    barrier = pltpu.get_barrier_semaphore()
    for peer, present, _ in sides:

        @pl.when(present)
        def _():
            pl.semaphore_signal(barrier, inc=1, device_id=peer, device_id_type=MESH)

    arrays = (
        (p_hbm, pv), (a_hbm, av), (fine_columns_hbm, fine_columns), (fine_counts_hbm, fine_counts),
        (prolong_columns_hbm, prolong_columns), (prolong_counts_hbm, prolong_counts),
    )
    p_in, a_in, *codes_in = [
        pltpu.make_async_copy(src, dst, in_sem.at[at]) for at, (src, dst) in enumerate(arrays)
    ]
    for copy in (*codes_in, p_in, a_in):
        copy.start()

    class Remote:
        def __init__(self, number, src, dst, side):
            peer, self.sends, self.receives = side
            self.copy = pltpu.make_async_remote_copy(
                src_ref=src,
                dst_ref=dst,
                send_sem=send_sem.at[number],
                recv_sem=recv_sem.at[number],
                device_id=peer,
                device_id_type=MESH,
            )

        def start(self):
            pl.when(self.sends)(self.copy.start)

        def wait_send(self):
            pl.when(self.sends)(self.copy.wait_send)

        def wait_recv(self):
            pl.when(self.receives)(self.copy.wait_recv)

    remote = Remote

    for (_, present, _), refs in (
        (up, (halo_t, got_u)),
        (down, (halo_b, got_d)),
        (left, (halo_l, corner_l, got_l)),
        (right, (halo_r, corner_r, got_r)),
    ):

        @pl.when(jnp.logical_not(present))
        def _():
            for ref in refs:
                ref[...] = jnp.zeros(ref.shape, ref.dtype)

    eye = (
        lax.broadcasted_iota(jnp.int32, (256, 256), 0)
        == lax.broadcasted_iota(jnp.int32, (256, 256), 1)
    ).astype(F32).astype(BF16)
    lane = lax.broadcasted_iota(jnp.int32, (1, 128), 1)
    line = lax.broadcasted_iota(jnp.int32, (16, 128), 0)
    half = lane < B

    def home_code(u, v, p):
        number = prolong_columns[u, v, p]
        code = (lax.bitwise_and(number, cols - 1) - col + 1) * 3 - row + 1
        code += lax.shift_right_logical(number, cols.bit_length() - 1)
        return jnp.where(p < prolong_counts[u, v], code, UNUSED)

    for copy in codes_in:
        copy.wait()
    codes = {(u, v): [home_code(u, v, p) for p in range(KP)] for u in range(AG) for v in range(AG)}

    def code_tile(ref, at, first, second):
        tile = jnp.zeros((16, 128), jnp.int32)
        for p in range(KP):
            tile = jnp.where(line == p, jnp.where(half, codes[first][p], codes[second][p]), tile)
        ref[KP * B :, at * 128 : (at + 1) * 128] = tile.astype(F32).astype(BF16)

    for u in range(AG):
        code_tile(ptx, 2 * u, (u, 0), (u, 3))
        code_tile(ptx, 2 * u + 1, (u, 1), (u, 2))
    for side, edge in ((0, edge_l), (AG - 1, edge_r)):
        code_tile(edge, 0, (0, side), (1, side))
        code_tile(edge, 1, (2, side), (3, side))
    p_in.wait()
    for side, edge in ((0, edge_l), (AG - 1, edge_r)):
        edge[0 : KP * B, :] = dot_nt(eye, pv[:, side].reshape(256, 256)).astype(BF16)
    for u in range(AG):
        ptx[0 : KP * B, u * 256 : (u + 1) * 256] = dot_nt(
            eye, jnp.concatenate([pv[u, v] for v in PLACES], axis=0)
        ).astype(BF16)

    pl.semaphore_wait(barrier, sum(present.astype(jnp.int32) for _, present, _ in sides))
    to_left = remote(0, edge_l, halo_r, left)
    to_right = remote(1, edge_r, halo_l, right)
    ends, inner = slice(0, 128), slice(128, 256)
    ends_up = remote(2, ptx.at[:, 0:128], halo_b.at[:, ends], up)
    ends_down = remote(3, ptx.at[:, 768:896], halo_t.at[:, ends], down)
    inner_up = remote(4, ptx.at[:, 128:256], halo_b.at[:, inner], up)
    inner_down = remote(5, ptx.at[:, 896:1024], halo_t.at[:, inner], down)
    for copy in (ends_up, ends_down, inner_up, inner_down, to_left, to_right):
        copy.start()

    def own_dense(u, carry):
        lanes = pl.ds(pl.multiple_of(u * 256, 256), 256)
        dense(
            ptx, lanes, 256,
            lambda d, s: [
                (pdt, term_row(d, s), lanes),
                (r_own, window_row(d + 2, s + 1), lanes),
            ],
            blank_rows(r_own, lanes, (0, 4)),
        )
        return carry

    lax.fori_loop(0, AG, own_dense, 0)
    for edge, ref in ((edge_l, pdt_l), (edge_r, pdt_r)):
        lanes = slice(0, 256)
        dense(edge, lanes, 256, lambda d, s: [(ref, term_row(d, s), lanes)], [])

    a_in.wait()
    tiles = ((1, 4), (2, 3))

    def toward_code(u, v, k):
        number = fine_columns[u, v, k]
        code = (lax.shift_right_logical(number, fine_cols.bit_length() - 1) - row * AG - u) * 3
        code += lax.bitwise_and(number, fine_cols - 1) - col * AG - v + 4
        return jnp.where(k < fine_counts[u, v], code, UNUSED)

    def strip(u, carry):
        for v in range(AG):
            wide = [av[u, v, :, 128 * t : 128 * (t + 1)] for t in range(4)]
            last = av[u, v, :, 512:576]
            wide.append(jnp.concatenate([last, jnp.zeros_like(last)], axis=1))
            wide = wide + [swapped(w).astype(BF16) for w in wide]
            wide = [w.reshape(4, 16, 128) for w in wide]
            codes = jnp.full((16, 128), UNUSED, jnp.int32)
            toward = [toward_code(u, v, k) for k in range(KA)] + [UNUSED]
            for t in range(5):
                one, two = toward[2 * t], toward[2 * t + 1]
                codes = jnp.where(line == t, jnp.where(half, one, two), codes)
                codes = jnp.where(line == t + 5, jnp.where(half, two, one), codes)
            def gathered(wanted, skip=()):
                match = jnp.where(codes == jnp.where(half, wanted[0], wanted[1]), 1.0, 0.0)
                total = None
                for t in range(10):
                    if t not in skip:
                        mask = jnp.broadcast_to(match[t : t + 1], (16, 128)).astype(BF16)
                        part = mask[None] * wide[t]
                        total = part if total is None else total + part
                return total.reshape(B, 128)

            for at, pair in enumerate(tiles):
                steps = [target - 1 - v for target in pair]
                for dr in (-1, 0, 1):
                    here = (u + dr + 1, pl.ds((1 - dr) * 256 + PLACES.index(v) * B, B), pl.ds(at * 128, 128))
                    wanted = [(dr + 1) * 3 + dc + 1 if abs(dc) <= 1 else 99 for dc in steps]
                    if wanted == [99, 99]:
                        aw[here] = jnp.zeros((B, 128), BF16)
                    else:
                        aw[here] = gathered(wanted)
            if v in (0, AG - 1):
                ref, dc = (aw_l, -1) if v == 0 else (aw_r, 1)
                for at, pair in enumerate(((0, 1), (2, 3), (-1, 4))):
                    steps = [target - u for target in pair]
                    wanted = [jnp.where(jnp.abs(dr) <= 1, (dr + 1) * 3 + dc + 1, 99) for dr in steps]
                    ref[pl.ds(u * B, B), at * 128 : (at + 1) * 128] = gathered(wanted)
        return carry

    lax.fori_loop(0, AG, strip, 0)

    for w in range(-1, AG + 1):
        low_u, high_u = max(w - 1, 0), min(w + 1, AG - 1)
        place = w if 0 <= w < AG else (AG if w < 0 else AG + 1)
        q_own[:, place * 256 : (place + 1) * 256] = dot_nn(
            pdt[:, low_u * 256 : (high_u + 1) * 256],
            aw[w + 1, (low_u - w + 1) * 256 : (high_u - w + 2) * 256, :],
        ).astype(BF16)
    q_l[...] = dot_nn(pdt_l[...], aw_l[...]).astype(BF16)
    q_r[...] = dot_nn(pdt_r[...], aw_r[...]).astype(BF16)

    def joined(ref, first, second, keep):
        for at in range(0, PT_ROWS, 16):
            one, two = first[at : at + 16, :].astype(F32), second[at : at + 16, :].astype(F32)
            one = one if keep[0] else pltpu.roll(one, B, 1)
            two = two if keep[1] else pltpu.roll(two, B, 1)
            ref[at : at + 16, :] = jnp.where(half, one, two).astype(BF16)

    ends_up.wait_recv()
    ends_down.wait_recv()
    joined(pass_l, halo_t.at[:, ends], halo_b.at[:, ends], (True, False))
    joined(pass_r, halo_t.at[:, ends], halo_b.at[:, ends], (False, True))
    corner_to_left = remote(24, pass_l, corner_r, left)
    corner_to_right = remote(25, pass_r, corner_l, right)
    corner_to_left.start()
    corner_to_right.start()
    halo_out = (
        ends_up, ends_down, inner_up, inner_down, to_left, to_right,
        corner_to_left, corner_to_right,
    )

    def add_terms(kind, q_ref, q_lanes, r_ref, r_lanes, base, first, fresh=False):
        ref, at, shift = (c_side, slice(0, 384), 0) if kind == "side" else (c_mid, slice(384, 576), B)
        for j in range(3):
            lane_at = base + shift + (j * 5 + first) * B
            row_at = window_row(first, j)
            if lane_at % 128:
                lane_at, row_at = lane_at - B, row_at - B
            part = dot_nt(q_ref[at, q_lanes], r_ref[row_at : row_at + 256, r_lanes])
            window = slice(lane_at, lane_at + 256)
            ref[:, window] = part if fresh else ref[:, window] + part

    def corner_terms(kind):
        corners = slice(256, 384)
        if kind == "side":
            c_side[:, 0:1024] += dot_nt(q_l[0:384, corners], r_l[64:1088, corners])
            c_side[:, 640:WIDE] += dot_nt(q_r[0:384, corners], r_r[64:1088, corners])
        else:
            c_mid[:, 0:1024] += dot_nt(q_l[384:576, corners], r_l[0:1024, corners])
            c_mid[:, 640:WIDE] += dot_nt(q_r[384:576, corners], r_r[0:1024, corners])

    own, over, under = slice(0, 1024), slice(1024, 1280), slice(1280, 1536)
    nearby = slice(0, 256)
    for ref, spans in (
        (c_side, ((0, 384), (896, 1024), (1280, WIDE))),
        (c_mid, ((0, 384), (640, 768), (1280, WIDE))),
    ):
        for lo, hi in spans:
            ref[:, lo:hi] = jnp.zeros((ref.shape[0], hi - lo), F32)
    add_terms("side", q_own, own, r_own, own, 5 * B, 1, True)

    to_left.wait_recv()
    to_right.wait_recv()
    for halo, ref in ((halo_l, r_l), (halo_r, r_r)):
        lanes = slice(0, 256)
        dense(
            halo, lanes, 256,
            lambda d, s: [(ref, window_row(d + 2, s + 1), lanes)],
            blank_rows(ref, lanes, (0, 4)),
        )
    add_terms("side", q_l, nearby, r_l, nearby, 0, 1)
    add_terms("side", q_r, nearby, r_r, nearby, 10 * B, 1)

    inner_up.wait_recv()
    inner_down.wait_recv()
    for halo, shift, blanks, first in ((halo_t, 1, (3, 4), 1024), (halo_b, 3, (0, 1), 1280)):
        at = slice(first, first + 256)
        dense(
            halo, slice(0, 256), 256,
            lambda d, s: [(r_own, window_row(d + shift, s + 1), at)],
            blank_rows(r_own, at, blanks),
        )
    add_terms("side", q_own, over, r_own, over, 5 * B, 0)
    add_terms("side", q_own, under, r_own, under, 5 * B, 2)

    corner_to_left.wait_recv()
    corner_to_right.wait_recv()
    for corner, ref in ((corner_l, r_l), (corner_r, r_r)):
        spread, blocks = slot_parts(corner, slice(0, 128), 128)
        for side in (-1, 0, 1):
            for j in range(5):
                above, below = j - 1, j - 3
                codes = [home(d, side) if abs(d) <= 1 else 99 for d in (above, below)]
                code = jnp.where(half, codes[0], codes[1]).astype(F32).astype(BF16)
                row_at = window_row(j, side + 1)
                ref[row_at : row_at + B, 256:384] = chosen(spread, blocks, range(KP), code)
        for row_at in (0, 16 * B):
            ref[row_at : row_at + B, 256:384] = jnp.zeros((B, 128), BF16)
    corner_terms("side")

    side_copies = []
    for q in range(CHUNKS):
        for h in range(2):
            at, first = slice(q * 32 + h * 16, q * 32 + h * 16 + 16), h * B + q * 16
            send_l[at, :] = c_side[first : first + 16, :].astype(BF16)
            send_r[at, :] = c_side[192 + first : 208 + first, :].astype(BF16)
        at = slice(q * 32, q * 32 + 32)
        pair = (
            remote(6 + 2 * q, send_l.at[at], got_r.at[at], left),
            remote(7 + 2 * q, send_r.at[at], got_l.at[at], right),
        )
        for copy in pair:
            copy.start()
        side_copies.append(pair)
    send_l[128:192, :] = c_side[128:192, :].astype(BF16)
    send_r[128:192, :] = c_side[320:384, :].astype(BF16)

    add_terms("mid", q_own, own, r_own, own, 5 * B, 1, True)
    add_terms("mid", q_l, nearby, r_l, nearby, 0, 1)
    add_terms("mid", q_r, nearby, r_r, nearby, 10 * B, 1)
    add_terms("mid", q_own, over, r_own, over, 5 * B, 0)
    add_terms("mid", q_own, under, r_own, under, 5 * B, 2)
    corner_terms("mid")

    def folded(got_at, mid_at, lo, hi):
        total = None
        for ref, at, first in ((got_l, got_at, 0), (c_mid, mid_at, 256), (got_r, got_at, 640)):
            if first <= lo and hi <= first + WIDE:
                part = ref[at, lo - first : hi - first].astype(F32)
                total = part if total is None else total + part
        return total

    spans = ((0, 256), (256, 640), (640, 1664), (1664, 1920), (1920, FULL))
    row_copies = []
    for q in range(CHUNKS):
        for copy in side_copies[q]:
            copy.wait_recv()
        for h in range(2):
            at, first = slice(q * 32 + h * 16, q * 32 + h * 16 + 16), h * B + q * 16
            for lo, hi in spans:
                send_rows[at, lo:hi] = folded(at, slice(first, first + 16), lo, hi).astype(BF16)
        at = slice(q * 16, q * 16 + 16)
        pair = (
            remote(16 + 2 * q, send_rows.at[q * 32 : q * 32 + 16], got_d.at[at], up),
            remote(17 + 2 * q, send_rows.at[q * 32 + 16 : q * 32 + 32], got_u.at[at], down),
        )
        for copy in pair:
            copy.start()
        row_copies.append(pair)
    at = slice(128, 192)
    side_copies.append(
        (
            remote(14, send_l.at[at], got_r.at[at], left),
            remote(15, send_r.at[at], got_l.at[at], right),
        )
    )
    for copy in side_copies[CHUNKS]:
        copy.start()
    for copy in side_copies[CHUNKS]:
        copy.wait_recv()
    for lo, hi in spans:
        e_mid[:, lo:hi] = folded(at, at, lo, hi)

    for q in range(CHUNKS):
        for copy in row_copies[q]:
            copy.wait_recv()
        rows_16 = slice(q * 16, q * 16 + 16)
        for s in range(7):
            for t in range(7):
                total = None
                for ref, j in ((got_u, s), (e_mid, s - 1), (got_d, s - 2)):
                    if 0 <= j < 5:
                        at = (t * 5 + j) * B
                        part = ref[rows_16, at : at + B].astype(F32)
                        total = part if total is None else total + part
                at = (s * 7 + t) * B
                out_ref[0, 0, rows_16, at : at + B] = total.astype(BF16)

    for copy in [*halo_out] + [copy for pair in side_copies + row_copies for copy in pair]:
        copy.wait_send()


def per_device(
    fine_blocks, fine_columns, fine_counts, prolong_blocks, prolong_columns, prolong_counts
):
    vmem = pl.BlockSpec(memory_space=pltpu.VMEM)
    hbm = pl.BlockSpec(memory_space=pltpu.HBM)
    return pl.pallas_call(
        kernel,
        out_shape=jax.ShapeDtypeStruct((1, 1, B, 49 * B), BF16),
        in_specs=[hbm] * 6,
        out_specs=vmem,
        scratch_shapes=[
            pltpu.SMEM((AG, AG, KA), jnp.int32),
            pltpu.SMEM((AG, AG), jnp.int32),
            pltpu.SMEM((AG, AG, KP), jnp.int32),
            pltpu.SMEM((AG, AG), jnp.int32),
            pltpu.VMEM((AG, AG, B, KP * B), BF16),
            pltpu.VMEM((AG, AG, B, KA * B), BF16),
            pltpu.VMEM((PT_ROWS, 1024), BF16),
            pltpu.VMEM((PT_ROWS, 256), BF16),
            pltpu.VMEM((PT_ROWS, 256), BF16),
            pltpu.VMEM((PT_ROWS, 256), BF16),
            pltpu.VMEM((PT_ROWS, 256), BF16),
            pltpu.VMEM((PT_ROWS, 256), BF16),
            pltpu.VMEM((PT_ROWS, 256), BF16),
            *[pltpu.VMEM((PT_ROWS, 128), BF16)] * 4,
            pltpu.VMEM((9 * B, 1024), BF16),
            pltpu.VMEM((9 * B, 256), BF16),
            pltpu.VMEM((9 * B, 256), BF16),
            pltpu.VMEM((6, 768, 256), BF16),
            pltpu.VMEM((256, 384), BF16),
            pltpu.VMEM((256, 384), BF16),
            pltpu.VMEM((9 * B, 1536), BF16),
            pltpu.VMEM((9 * B, 384), BF16),
            pltpu.VMEM((9 * B, 384), BF16),
            pltpu.VMEM((R_ROWS, 1536), BF16),
            pltpu.VMEM((R_ROWS, 384), BF16),
            pltpu.VMEM((R_ROWS, 384), BF16),
            pltpu.VMEM((6 * B, WIDE), F32),
            pltpu.VMEM((3 * B, WIDE), F32),
            pltpu.VMEM((3 * B, WIDE), BF16),
            pltpu.VMEM((3 * B, WIDE), BF16),
            pltpu.VMEM((3 * B, WIDE), BF16),
            pltpu.VMEM((3 * B, WIDE), BF16),
            pltpu.VMEM((2 * B, FULL), BF16),
            pltpu.VMEM((B, FULL), F32),
            pltpu.VMEM((B, FULL), BF16),
            pltpu.VMEM((B, FULL), BF16),
            pltpu.SemaphoreType.DMA((6,)),
            pltpu.SemaphoreType.DMA((26,)),
            pltpu.SemaphoreType.DMA((26,)),
        ],
        compiler_params=pltpu.CompilerParams(
            collective_id=0, has_side_effects=True, vmem_limit_bytes=62 * 2**20
        ),
    )(
        prolong_blocks, fine_blocks,
        fine_columns, fine_counts, prolong_columns, prolong_counts,
    )


def solution(mesh):
    in_specs = (
        P("row", "col", None, None),
        P("row", "col", None),
        P("row", "col"),
        P("row", "col", None, None),
        P("row", "col", None),
        P("row", "col"),
    )
    return jax.shard_map(
        per_device,
        mesh=mesh,
        in_specs=in_specs,
        out_specs=P("row", "col", None, None),
        check_vma=False,
    )
```
